128 devices in a mesh: band: 8 (over y, core), wave: 8 (over z, x_lo), lev: 2 (over x_hi).
Axes of the slice: x: 4 (x_hi: 2, x_lo: 2; x = x_hi * 2 + x_lo), y: 4, z: 4, core: 2. Of those that a mesh axis runs over, the one named last changes fastest.
Arguments:
- fourier: float32 [2560, 96, 2, 4, 128], P('band', 'wave', None, None, 'lev'), may hold values from -6 to 6
- legendre: float32 [96, 1280, 2, 648], P('wave', 'band'), may hold values from -0.25 to 0.25
- pair_m: int32 [96], P('wave'), may hold values from 0 to 639, as said below
- mirror: int32 [2560], replicated, may hold values from 0 to 2559, as said below
Outputs:
- coefficients: float32 [96, 2, 4, 128, 648], P('wave', None, None, 'lev', 'band')
- energy: float32 [1279], replicated
The draws below stay inside these ranges and needn't reach their ends.
Inputs may be any that keep to these rules, and one draw needn't show every extreme that they name: `pair_m`: values are distinct and both 0 and 639 appear. mirror is an involution; every row of band block b < 8/2 (blocks of 320 rows) is paired with a row of block b + 4.
All inputs are finite; a program needn't handle non-finite values.
Results may differ from the reference program's by a relative error of at most 0.0003.
Values sent between devices are 32-bit elements; how exact they have to be, the bound alone decides.
No kernel may reach another device: no remote copies, remote signals or barrier semaphores. Data moves between devices by JAX's collectives and lax.ppermute only.
A program may use at most 192 MiB of HBM per device.

```python
import jax
import jax.numpy as jnp
from jax import lax

NLAT = 2560
NDEG = 1280
CP = 648
LEV = 128
PAIRS = 96
LAT_DEV = 320
N_BAND = 8


def draw_pair_m(key, part):
    key = jax.random.fold_in(key, 11)
    first_key, second_key = jax.random.split(key)
    count = NDEG // 2
    others = jax.random.permutation(first_key, count - 2)[:PAIRS - 2] + 1
    values = jnp.concatenate([jnp.array([0, count - 1], jnp.int32), others.astype(jnp.int32)])
    return values[jax.random.permutation(second_key, PAIRS)]


def draw_mirror(key, part):
    key = jax.random.fold_in(key, 23)
    blocks = NLAT // 2 // LAT_DEV
    keys = jax.random.split(key, blocks)
    orders = jax.vmap(lambda single: jax.random.permutation(single, LAT_DEV))(keys).astype(jnp.int32)
    offsets = (jnp.arange(blocks, dtype=jnp.int32)[:, None] + blocks) * LAT_DEV
    partner = (orders + offsets).reshape(-1)
    north = jnp.arange(NLAT // 2, dtype=jnp.int32)
    mapping = jnp.zeros((NLAT,), jnp.int32)
    mapping = mapping.at[north].set(partner)
    mapping = mapping.at[partner].set(north)
    return mapping


def raised(values, rng, source, target, parts, factor):
    owner, partner = [(jnp.arange(values.shape[axis_at]) // (values.shape[axis_at] // parts)).reshape([-1 if axis == axis_at else 1 for axis in range(values.ndim)]) for axis_at in (source, target)]
    chosen = jax.random.permutation(rng, parts)[partner]
    strong = (owner == chosen) | (owner == (partner + parts // 2) % parts)
    return jnp.where(strong, factor * values, values)


def levels(stream_key, extent, shards, least, largest):
    factor_of, own = 1.0, jax.random.fold_in(stream_key, 6)
    for position, parts in shards:
        heights = jnp.exp(jax.random.uniform(jax.random.fold_in(own, position), (parts,), jnp.float32, least / len(shards), largest / len(shards)))
        factor_of = factor_of * jnp.repeat(heights, extent[position] // parts).reshape([-1 if axis == position else 1 for axis in range(len(extent))])
    return factor_of


def noise(rng, dims, spread, most, pieces=(), held_as=jnp.bfloat16):
    values = spread * jax.random.normal(rng, dims, jnp.float32)
    if pieces:
        values = values * levels(rng, dims, pieces, -0.22, 0.18)
    return jnp.clip(values, -most, most).astype(held_as)


def heavy_noise(own_key, dims, width, bound, shards, heavy, held_as=jnp.bfloat16):
    values = width * jax.random.normal(own_key, dims, jnp.float32)
    if shards:
        values = values * levels(own_key, dims, shards, -0.22, 0.18)
    return jnp.clip(raised(values, jax.random.fold_in(own_key, 3), *heavy), -bound, bound).astype(held_as)


def setup_inputs(seed: int = 0) -> dict:
    splits = jax.random.split(jax.random.key(seed), 5)
    return {
        "fourier": noise(splits[0], (NLAT, PAIRS, 2, 4, LEV), 1.0, 6.0, ((0, 8), (1, 8), (4, 2)), jnp.float32),
        "legendre": heavy_noise(splits[1], (PAIRS, NLAT // 2, 2, CP), (NLAT // 2) ** -0.5, 0.25, ((0, 8), (1, 8)), (1, 3, 8, 2.0), jnp.float32),
        "pair_m": draw_pair_m(jax.random.fold_in(splits[4], 71), 0),
        "mirror": draw_mirror(jax.random.fold_in(splits[4], 71), 0),
    }


def slot_layout(wavenum, slots):
    first_m = wavenum[:, None, None]
    parity = jnp.arange(2, dtype=jnp.int32)[None, :, None]
    column = jnp.arange(slots, dtype=jnp.int32)[None, None, :]
    count_first = (NDEG - first_m - parity + 1) // 2
    leading = column < count_first
    second_m = NDEG - 1 - first_m
    degree = jnp.where(leading, first_m + parity + 2 * column, second_m + parity + 2 * (column - count_first))
    owner_m = jnp.where(leading, first_m, second_m)
    return leading, degree, owner_m


def degree_energy(squares, degree, owner_m):
    usable = (degree >= 1) & (degree <= NDEG - 1)
    safe = jnp.maximum(degree, 1).astype(jnp.float32)
    factor = jnp.where(owner_m == 0, 1.0, 2.0).astype(jnp.float32)
    term = jnp.where(usable, factor * squares / (4.0 * safe * (safe + 1.0)), 0.0)
    bins = jnp.where(usable, degree - 1, NDEG - 1).astype(jnp.int32)
    summed = jax.ops.segment_sum(term.reshape(-1), bins.reshape(-1), num_segments=NDEG)
    return summed[:NDEG - 1]


def reference(fourier, legendre, pair_m, mirror):
    half_rows = LAT_DEV // 2
    half_bands = N_BAND // 2
    pair_row = jnp.arange(NLAT // 2, dtype=jnp.int32)
    block = pair_row // half_rows
    north = (block % half_bands) * LAT_DEV + (block // half_bands) * half_rows + pair_row % half_rows
    south = mirror[north]
    leading, degree, owner_m = slot_layout(pair_m, CP)

    def one_pair(index):
        field = fourier[:, index]
        north_f = field[north]
        south_f = field[south]
        results = []
        for parity, folded in ((0, north_f + south_f), (1, north_f - south_f)):
            flat = folded.reshape(NLAT // 2, -1)
            result = jnp.dot(flat.T, legendre[index, :, parity, :], precision=lax.Precision.HIGHEST,
                             preferred_element_type=jnp.float32)
            result = result.reshape(2, 4, LEV, CP)
            pick = leading[index, parity][None, None, :]
            valid = (degree[index, parity] <= NDEG - 1)[None, None, :]
            results.append(jnp.where(valid, jnp.where(pick, result[0], result[1]), 0.0))
        return jnp.stack(results)

    coefficients = lax.map(one_pair, jnp.arange(PAIRS, dtype=jnp.int32))
    squares = jnp.sum(coefficients * coefficients, axis=(2, 3))
    energy = jnp.log(degree_energy(squares, degree, owner_m))
    return coefficients, energy
```

```python
import functools

import jax
import jax.numpy as jnp
from jax import lax
from jax.experimental import pallas as pl
from jax.experimental.pallas import tpu as pltpu
from jax.sharding import PartitionSpec as P

NDEG = 1280
CHUNKS = 3
F32 = jnp.float32
BF16 = jnp.bfloat16
VMEM_LIMIT = 48 * 1024 * 1024


def split_two(x):
    high = x.astype(BF16)
    low = (x - high.astype(F32)).astype(BF16)
    return high, low


def dot_nt(a, b):
    return lax.dot_general(a, b, (((1,), (1,)), ((), ())), preferred_element_type=F32)


def dot_nn(a, b):
    return jnp.dot(a, b, preferred_element_type=F32)


def send_along(x, up, cross):
    size = lax.axis_size("band")
    chips = size // 2
    pairs = [(i, ((i // 2 + up) % chips) * 2 + ((i % 2) ^ cross)) for i in range(size)]
    return lax.ppermute(x, "band", pairs)


def pick_kernel(place_ref, index_ref, field_ref, own_ref, cross_ref, *, own_steps):
    step = pl.program_id(0)
    count = index_ref.shape[0]
    rows = field_ref.shape[2]
    lanes = lax.broadcasted_iota(jnp.int32, (count, rows), 1)
    chosen = jnp.where(index_ref[...] == lanes, 1.0, 0.0).astype(BF16)
    high, low = split_two(field_ref[0])
    picked = dot_nt(chosen, high) + dot_nt(chosen, low)

    @pl.when(step < own_steps)
    def _():
        own_ref[0] = picked

    @pl.when(step >= own_steps)
    def _():
        cross_ref[0] = picked


def pick_rows(place, index, field, chunk, chunks):
    pairs, width, rows = field.shape
    group = pairs // 2
    each = group // chunks
    count = index.shape[0]

    def field_map(step, place_ref):
        mine = step < each
        core = jnp.where(mine, place_ref[0], 1 - place_ref[0])
        return (core * group + chunk * each + jnp.where(mine, step, step - each), 0, 0)

    shape = jax.ShapeDtypeStruct((each, count, width), F32)
    return pl.pallas_call(
        functools.partial(pick_kernel, own_steps=each),
        grid_spec=pltpu.PrefetchScalarGridSpec(
            num_scalar_prefetch=1,
            grid=(2 * each,),
            in_specs=[
                pl.BlockSpec((count, 1), lambda step, place_ref: (0, 0)),
                pl.BlockSpec((1, width, rows), field_map),
            ],
            out_specs=[
                pl.BlockSpec((1, count, width), lambda step, place_ref: (jnp.minimum(step, each - 1), 0, 0)),
                pl.BlockSpec((1, count, width), lambda step, place_ref: (jnp.maximum(step - each, 0), 0, 0)),
            ],
        ),
        out_shape=[shape, shape],
        compiler_params=pltpu.CompilerParams(vmem_limit_bytes=VMEM_LIMIT),
        cost_estimate=pl.CostEstimate(
            flops=8 * each * count * width * rows,
            bytes_accessed=2 * each * width * (rows + count) * 4,
            transcendentals=0,
        ),
        name="pick_rows",
    )(place, index, field)


def layout_kernel(*refs, share):
    out_ref = refs[-1]
    tiles = (len(refs) - 1) // 2
    half = refs[0].shape[1] // 2
    main = lanes = 128
    rest = 2 * main - 6 * (half - main)
    for parity in range(2):
        for tile in range(tiles):
            own_high, own_low = split_two(refs[tile][0, pl.ds(parity, half, stride=2), :])
            cross_high, cross_low = split_two(refs[tiles + tile][0, pl.ds(parity, half, stride=2), :])
            tail_high = [own_high[main:], cross_high[main:]]
            tail_low = [own_low[main:], cross_low[main:]]
            blocks = (
                [own_high[:main], cross_high[:main]],
                [own_low[:main], cross_low[:main]],
                tail_high + tail_high + tail_low + [jnp.zeros((rest, lanes), BF16)],
            )
            for i, block in enumerate(blocks):
                turned = jnp.concatenate(block, 0).T
                for s in range(out_ref.shape[2]):
                    first = max(s * share, tile * lanes)
                    last = min((s + 1) * share, (tile + 1) * lanes)
                    if first < last:
                        out_ref[0, parity, s, first - s * share : last - s * share, 2 * main * i : 2 * main * (i + 1)] = (
                            turned[first - tile * lanes : last - tile * lanes]
                        )


def lay_out(own, cross, share, padded):
    pairs, rows, slots = own.shape
    shares = slots // share
    tiles = (slots + 127) // 128

    def block(tile):
        return pl.BlockSpec((1, rows, 128), lambda step: (step, 0, tile))

    return pl.pallas_call(
        functools.partial(layout_kernel, share=share),
        grid=(pairs,),
        in_specs=[block(tile) for tile in range(tiles)] * 2,
        out_specs=pl.BlockSpec((1, 2, shares, padded, 768), lambda step: (step, 0, 0, 0, 0)),
        out_shape=jax.ShapeDtypeStruct((pairs, 2, shares, padded, 768), BF16),
        compiler_params=pltpu.CompilerParams(vmem_limit_bytes=VMEM_LIMIT),
        cost_estimate=pl.CostEstimate(
            flops=0, bytes_accessed=pairs * (2 * rows * slots * 4 + 2 * shares * padded * 768 * 2), transcendentals=0
        ),
        name="lay_out",
    )(*[own] * tiles, *[cross] * tiles)


def project_kernel(
    place_ref, wave_ref, keep_ref, recv_ref, keep_x_ref, recv_x_ref, table_ref, *refs, share, chunk, chunks
):
    outs, (high_ref, low_ref, tail_ref) = refs[:8], refs[8:]
    step = pl.program_id(0)
    each = pl.num_programs(0)
    group = each * chunks
    core = place_ref[0]
    chip = place_ref[1]
    chips = place_ref[2]
    first_m = wave_ref[core * group + chunk * each + step]
    half = keep_ref.shape[1]
    width = keep_ref.shape[2] // 2
    main = 128
    tail = half - main
    padded = table_ref.shape[3]
    side = jnp.where(chip < chips // 2, 1.0, -1.0)
    for parity in range(2):
        for j, (keep, recv) in enumerate(((keep_ref, recv_ref), (keep_x_ref, recv_x_ref))):
            if parity == 0:
                folded = keep[0] + recv[0]
            else:
                folded = side * (keep[0] - recv[0])
            high, low = split_two(folded)
            for member in range(2):
                part = slice(member * width, (member + 1) * width)
                high_ref[member, j * main : (j + 1) * main] = high[:main, part]
                low_ref[member, j * main : (j + 1) * main] = low[:main, part]
                for k, value in enumerate((high, low, high)):
                    at = (2 * k + j) * tail
                    tail_ref[member, at : at + tail] = value[main:, part]
        used = 6 * tail
        for member in range(2):
            tail_ref[member, used:] = jnp.zeros((2 * main - used, width), BF16)
        count = (NDEG - first_m - parity + 1) // 2
        for position in range(8):
            ahead, other = position // 2, position % 2
            owner = lax.rem(chip + ahead, chips)
            which = 2 * owner + jnp.where(other == 1, 1 - core, core)
            start = which * share
            out_ref = outs[position]

            def product(member):
                table = table_ref[0, parity, which]
                high_part = table[:, : 2 * main]
                return (
                    dot_nn(high_part, high_ref[member])
                    + dot_nn(high_part, low_ref[member])
                    + dot_nn(table[:, 2 * main : 4 * main], high_ref[member])
                    + dot_nn(table[:, 4 * main :], tail_ref[member])
                )

            slot = start + lax.broadcasted_iota(jnp.int32, (padded, width), 0)
            leading = slot < count
            valid = leading | (parity + 2 * (slot - count) <= first_m)
            main_member = jnp.where(start >= count, 1, 0)
            value = jnp.where(valid, product(main_member), 0.0)
            mixed = (start < count) & (start + share > count)
            for unit in range(each_static(refs, share)):
                if unit % 2 != parity:
                    continue
                rows = slice(unit * share, (unit + 1) * share)

                @pl.when(step == unit // 2)
                def _():
                    out_ref[rows, :] = value[:share]

                    @pl.when(mixed)
                    def _():
                        other_value = jnp.where(valid, product(1), 0.0)
                        out_ref[rows, :] = jnp.where(leading, value, other_value)[:share]


def each_static(refs, share):
    return refs[0].shape[0] // share


def project(place, wave, keep, recv, keep_x, recv_x, table, share, chunk, chunks):
    each, half, width = keep.shape
    rows = 2 * each * share
    rows = (rows + 7) // 8 * 8
    padded, depth = table.shape[3:]
    field = pl.BlockSpec((1, half, width), lambda step, *_: (step, 0, 0))
    table_spec = pl.BlockSpec((1,) + table.shape[1:], lambda step, *_: (chunk * each + step, 0, 0, 0, 0))
    out = pl.BlockSpec((rows, width // 2), lambda step, *_: (0, 0))
    scratch = pltpu.VMEM((2, 256, width // 2), BF16)
    return pl.pallas_call(
        functools.partial(project_kernel, share=share, chunk=chunk, chunks=chunks),
        grid_spec=pltpu.PrefetchScalarGridSpec(
            num_scalar_prefetch=2,
            grid=(each,),
            in_specs=[field, field, field, field, table_spec],
            out_specs=[out] * 8,
            scratch_shapes=[scratch, scratch, scratch],
        ),
        out_shape=[jax.ShapeDtypeStruct((rows, width // 2), F32)] * 8,
        compiler_params=pltpu.CompilerParams(vmem_limit_bytes=VMEM_LIMIT),
        cost_estimate=pl.CostEstimate(
            flops=2 * each * 2 * 9 * padded * 1024 * width // 2,
            bytes_accessed=each * (4 * half * width * 4 + 16 * padded * depth * 2 + 16 * share * width * 2),
            transcendentals=0,
        ),
        name="project",
    )(place, wave, keep, recv, keep_x, recv_x, table)


def finish_kernel(place_ref, wave_ref, *refs, share, chunk, chunks):
    parts, (out_ref, energy_ref) = refs[:6], refs[-2:]
    step = pl.program_id(0)
    each = out_ref.shape[0]
    group = each * chunks
    core = place_ref[0]
    which = 2 * place_ref[1] + core
    start = which * share
    lanes = 128
    for side in range(2):

        @pl.when(step == side)
        def _():
            terms = []
            spots = []
            for pair in range(each):
                first_m = wave_ref[(core if side == 0 else 1 - core) * group + chunk * each + pair]
                for parity in range(2):
                    unit = 2 * pair + parity
                    rows = slice(unit * share, (unit + 1) * share)
                    a, b, c = (part[rows, :] for part in parts[3 * side : 3 * side + 3])
                    value = (a + b + c).T
                    out_ref[pair, parity] = value.reshape(out_ref.shape[2:])
                    squares = jnp.sum(value * value, axis=0, keepdims=True)
                    squares = jnp.concatenate([squares, jnp.zeros((1, lanes - share), F32)], 1)
                    column = lax.broadcasted_iota(jnp.int32, (1, lanes), 1)
                    slot = start + column
                    count = (NDEG - first_m - parity + 1) // 2
                    leading = slot < count
                    second_m = NDEG - 1 - first_m
                    degree = jnp.where(leading, first_m + parity + 2 * slot, second_m + parity + 2 * (slot - count))
                    owner_m = jnp.where(leading, first_m, second_m)
                    usable = (column < share) & (degree >= 1) & (degree <= NDEG - 1)
                    safe = jnp.maximum(degree, 1).astype(F32)
                    factor = jnp.where(owner_m == 0, 1.0, 2.0)
                    terms.append(jnp.where(usable, factor * squares / (4.0 * safe * (safe + 1.0)), 0.0))
                    spots.append(jnp.where(usable, degree - 1, 0))
            term = jnp.concatenate(terms, 1)
            spot = jnp.concatenate(spots, 1)
            size = term.shape[1]
            band = lax.broadcasted_iota(jnp.int32, (16, size), 0)
            left = jnp.where(spot // lanes == band, term, 0.0)
            line = lax.broadcasted_iota(jnp.int32, (lanes, size), 0)
            right = jnp.where(spot % lanes == line, 1.0, 0.0).astype(BF16)
            first = left.astype(BF16)
            rest = left - first.astype(F32)
            second = rest.astype(BF16)
            third = (rest - second.astype(F32)).astype(BF16)
            total = dot_nt(first, right) + dot_nt(second, right) + dot_nt(third, right)
            if side == 0:
                energy_ref[...] = total
            else:
                energy_ref[...] += total


def finish(place, wave, parts, held, shape, share, chunk, chunks):
    pairs = shape[0]
    group = pairs // 2
    each = group // chunks
    rows, width = parts[0].shape

    def out_map(step, place_ref, wave_ref):
        core = jnp.where(step == 0, place_ref[0], 1 - place_ref[0])
        return (core * chunks + chunk, 0, 0, 0, 0)

    full = pl.BlockSpec((rows, width), lambda step, *_: (0, 0))
    operands = list(parts)
    in_specs = [full] * 6
    aliases = {}
    if held is not None:
        operands.append(held)
        in_specs.append(pl.BlockSpec(memory_space=pl.ANY))
        aliases = {8: 0}
    return pl.pallas_call(
        functools.partial(finish_kernel, share=share, chunk=chunk, chunks=chunks),
        grid_spec=pltpu.PrefetchScalarGridSpec(
            num_scalar_prefetch=2,
            grid=(2,),
            in_specs=in_specs,
            out_specs=[
                pl.BlockSpec((each,) + shape[1:], out_map),
                pl.BlockSpec((16, 128), lambda step, *_: (0, 0)),
            ],
        ),
        out_shape=[jax.ShapeDtypeStruct(shape, F32), jax.ShapeDtypeStruct((16, 128), F32)],
        input_output_aliases=aliases,
        compiler_params=pltpu.CompilerParams(vmem_limit_bytes=VMEM_LIMIT),
        cost_estimate=pl.CostEstimate(
            flops=10 * 6 * rows * width, bytes_accessed=10 * rows * width * 4, transcendentals=0
        ),
        name="finish",
    )(place, wave, *operands)


def all_sum(x):
    for axis, bit in (("band", 1), ("lev", 1), ("wave", 1), ("wave", 2), ("band", 2), ("wave", 4), ("band", 4)):
        size = lax.axis_size(axis)
        x = x + lax.ppermute(x, axis, [(i, i ^ bit) for i in range(size)])
    return x


def shards(fourier, legendre, pair_m, mirror):
    bands = lax.axis_size("band")
    chips = bands // 2
    rows, pairs, members, comps, levs = fourier.shape
    half_rows = rows // 2
    slots = legendre.shape[3]
    share = slots // bands
    padded = (share + 15) // 16 * 16
    position = lax.axis_index("band")
    chip, core = position // 2, position % 2
    place = jnp.stack([core, chip, jnp.int32(chips)]).astype(jnp.int32)

    north_base = position % chips * rows
    south_base = north_base + chips * rows
    partner = lax.dynamic_slice(mirror, (north_base,), (rows,)) - south_base
    plain = (jnp.arange(rows, dtype=jnp.int32) + half_rows) % rows
    index = jnp.where(position < chips, plain, partner).reshape(rows, 1)
    send_index, keep_index = index[:half_rows], index[half_rows:]
    field = jnp.transpose(fourier, (1, 2, 3, 4, 0)).reshape(pairs, members * comps * levs, rows)

    received = []
    for chunk in range(CHUNKS):
        own, cross = pick_rows(place, send_index, field, chunk, CHUNKS)
        received.append((send_along(own, chips // 2, 0), send_along(cross, chips // 2, 1)))

    group = pairs // 2
    table = legendre.reshape(pairs, rows, slots)
    own_table = lax.dynamic_slice_in_dim(table, core * group, group, 0)
    cross_table = send_along(lax.dynamic_slice_in_dim(table, (1 - core) * group, group, 0), 0, 1)
    kept, kept_cross = pick_rows(place, keep_index, field, 0, 1)
    kept_cross = send_along(kept_cross, 0, 1)
    table = lay_out(own_table, cross_table, share, padded)

    each = group // CHUNKS
    done = []
    for chunk in range(CHUNKS):
        here = slice(chunk * each, (chunk + 1) * each)
        mine, mine_x, up, up_x, far, far_x, down, down_x = project(
            place, pair_m, kept[here], received[chunk][0], kept_cross[here], received[chunk][1],
            table, share, chunk, CHUNKS,
        )
        far = send_along(far, 1, 0)
        far_x = send_along(far_x, -1, 0)
        up_x = send_along(up_x, 1, 1)
        down = send_along(down, -1, 0)
        mine_x = send_along(mine_x, 0, 1)
        up = send_along(up + far, 1, 0)
        down_x = send_along(down_x + far_x, -1, 1)
        done.append((mine, up, down, mine_x, up_x, down_x))

    shape = (pairs, 2, comps, levs, share)
    held = None
    energies = []
    for chunk in range(CHUNKS):
        held, energy = finish(place, pair_m, done[chunk], held, shape, share, chunk, CHUNKS)
        energies.append(energy)
    total = all_sum(functools.reduce(jnp.add, energies))
    return (held, jnp.log(total.reshape(-1)[: NDEG - 1]))


def solution(mesh):
    return jax.shard_map(
        shards,
        mesh=mesh,
        in_specs=(
            P("band", "wave", None, None, "lev"),
            P("wave", "band", None, None),
            P("wave"),
            P(),
        ),
        out_specs=(P("wave", None, None, "lev", "band"), P()),
        check_vma=False,
    )
```

```python
import functools

import jax
import jax.numpy as jnp
from jax import lax
from jax.experimental import pallas as pl
from jax.experimental.pallas import tpu as pltpu
from jax.sharding import PartitionSpec as P

NDEG = 1280
CHUNKS = 3
F32 = jnp.float32
BF16 = jnp.bfloat16
VMEM_LIMIT = 48 * 1024 * 1024


def behind(x, after):
    return lax.optimization_barrier((x, after))[0]


def split_two(x):
    high = x.astype(BF16)
    low = (x - high.astype(F32)).astype(BF16)
    return high, low


def dot_nt(a, b):
    return lax.dot_general(a, b, (((1,), (1,)), ((), ())), preferred_element_type=F32)


def dot_nn(a, b):
    return jnp.dot(a, b, preferred_element_type=F32)


def send_along(x, up, cross):
    size = lax.axis_size("band")
    chips = size // 2
    pairs = [(i, ((i // 2 + up) % chips) * 2 + ((i % 2) ^ cross)) for i in range(size)]
    return lax.ppermute(x, "band", pairs)


def pick_kernel(place_ref, index_ref, field_ref, out_ref):
    count = index_ref.shape[0]
    rows = field_ref.shape[2]
    lanes = lax.broadcasted_iota(jnp.int32, (count, rows), 1)
    chosen = jnp.where(index_ref[...] == lanes, 1.0, 0.0).astype(BF16)
    high, low = split_two(field_ref[0])
    out_ref[0] = dot_nt(chosen, high) + dot_nt(chosen, low)


def pick_rows(place, index, field, chunk, chunks):
    pairs, width, rows = field.shape
    each = pairs // chunks
    count = index.shape[0]

    def field_map(step, place_ref):
        return (chunk * each + step, 0, 0)

    return pl.pallas_call(
        pick_kernel,
        grid_spec=pltpu.PrefetchScalarGridSpec(
            num_scalar_prefetch=1,
            grid=(each,),
            in_specs=[
                pl.BlockSpec((count, 1), lambda step, place_ref: (0, 0)),
                pl.BlockSpec((1, width, rows), field_map),
            ],
            out_specs=pl.BlockSpec((1, count, width), lambda step, place_ref: (step, 0, 0)),
        ),
        out_shape=jax.ShapeDtypeStruct((each, count, width), F32),
        compiler_params=pltpu.CompilerParams(vmem_limit_bytes=VMEM_LIMIT),
        cost_estimate=pl.CostEstimate(
            flops=4 * each * count * width * rows,
            bytes_accessed=each * width * (rows + count) * 4,
            transcendentals=0,
        ),
        name="pick_rows",
    )(place, index, field)


def layout_kernel(*refs, share):
    out_ref = refs[-1]
    lanes = main = 128
    half = refs[0].shape[1]
    rest = main - 3 * (half - main)
    for parity in range(2):
        for tile, ref in enumerate(refs[:-1]):
            high, low = split_two(ref[0, :, parity, :])
            blocks = (
                high[:main],
                low[:main],
                jnp.concatenate([high[main:], high[main:], low[main:], jnp.zeros((rest, lanes), BF16)], 0),
            )
            for i, block in enumerate(blocks):
                turned = block.T
                for s in range(out_ref.shape[2]):
                    first = max(s * share, tile * lanes)
                    last = min((s + 1) * share, (tile + 1) * lanes)
                    if first < last:
                        out_ref[0, parity, s, first - s * share : last - s * share, main * i : main * (i + 1)] = turned[
                            first - tile * lanes : last - tile * lanes
                        ]


def lay_out(table, share, padded):
    pairs, half, _, slots = table.shape
    shares = slots // share
    tiles = (slots + 127) // 128

    def block(tile):
        return pl.BlockSpec((1, half, 2, 128), lambda step: (step, 0, 0, tile))

    return pl.pallas_call(
        functools.partial(layout_kernel, share=share),
        grid=(pairs,),
        in_specs=[block(tile) for tile in range(tiles)],
        out_specs=pl.BlockSpec((1, 2, shares, padded, 384), lambda step: (step, 0, 0, 0, 0)),
        out_shape=jax.ShapeDtypeStruct((pairs, 2, shares, padded, 384), BF16),
        compiler_params=pltpu.CompilerParams(vmem_limit_bytes=VMEM_LIMIT),
        cost_estimate=pl.CostEstimate(
            flops=0, bytes_accessed=pairs * (2 * half * slots * 4 + 2 * shares * padded * 384 * 2), transcendentals=0
        ),
        name="lay_out",
    )(*[table] * tiles)


def project_kernel(
    place_ref, wave_ref, keep_ref, recv_ref, table_ref, mine_ref, far_ref, cross_ref, both_ref, mixed_ref, *, share, chunk
):
    step = pl.program_id(0)
    each = pl.num_programs(0)
    core = place_ref[0]
    chip = place_ref[1]
    chips = place_ref[2]
    first_m = wave_ref[chunk * each + step]
    half = keep_ref.shape[1]
    width = keep_ref.shape[2] // 2
    main = 128
    tail = half - main
    padded = table_ref.shape[3]
    units = mine_ref.shape[0] // (table_ref.shape[2] // 2 * share)
    side = jnp.where(chip < chips // 2, 1.0, -1.0)
    for parity in range(2):
        if parity == 0:
            folded = keep_ref[0] + recv_ref[0]
        else:
            folded = side * (keep_ref[0] - recv_ref[0])
        high, low = split_two(folded)
        for member in range(2):
            part = slice(member * width, (member + 1) * width)
            both_ref[member, :main] = high[:main, part]
            both_ref[member, main:] = low[:main, part]
            mixed_ref[member, :main] = high[:main, part]
            for k, value in enumerate((high, low, high)):
                at = main + k * tail
                mixed_ref[member, at : at + tail] = value[main:, part]
            mixed_ref[member, main + 3 * tail :] = jnp.zeros((main - 3 * tail, width), BF16)
        count = (NDEG - first_m - parity + 1) // 2
        for position in range(table_ref.shape[2]):
            ahead, other = position // 2, position % 2
            owner = lax.rem(chip + ahead, chips)
            which = 2 * owner + jnp.where(other == 1, 1 - core, core)
            start = which * share
            out_ref, place_at = mine_ref, ahead
            if other:
                out_ref, place_at = (far_ref, 0) if ahead == 2 else (cross_ref, min(ahead, 2))

            def product(member):
                table = table_ref[0, parity, which]
                high_part = table[:, :main]
                return dot_nn(jnp.concatenate([high_part, high_part], 1), both_ref[member]) + dot_nn(
                    table[:, main:], mixed_ref[member]
                )

            slot = start + lax.broadcasted_iota(jnp.int32, (padded, width), 0)
            leading = slot < count
            valid = leading | (parity + 2 * (slot - count) <= first_m)
            main_member = jnp.where(start >= count, 1, 0)
            value = jnp.where(valid, product(main_member), 0.0)
            mixed = (start < count) & (start + share > count)
            for unit in range(parity, units, 2):
                rows = slice((place_at * units + unit) * share, (place_at * units + unit + 1) * share)

                @pl.when(step == unit // 2)
                def _():
                    out_ref[rows, :] = value[:share]

                    @pl.when(mixed)
                    def _():
                        second = jnp.where(valid, product(1), 0.0)
                        out_ref[rows, :] = jnp.where(leading, value, second)[:share]


def project(place, wave, keep, recv, table, share, chunk):
    each, half, width = recv.shape
    shares, padded, depth = table.shape[2:]
    rows = 2 * each * share
    sizes = [rows * shares // 2, rows, rows * (shares // 2 - 1)]
    scratch = pltpu.VMEM((2, 256, width // 2), BF16)
    return pl.pallas_call(
        functools.partial(project_kernel, share=share, chunk=chunk),
        grid_spec=pltpu.PrefetchScalarGridSpec(
            num_scalar_prefetch=2,
            grid=(each,),
            in_specs=[
                pl.BlockSpec((1, half, width), lambda step, *_: (chunk * each + step, 0, 0)),
                pl.BlockSpec((1, half, width), lambda step, *_: (step, 0, 0)),
                pl.BlockSpec((1,) + table.shape[1:], lambda step, *_: (chunk * each + step, 0, 0, 0, 0)),
            ],
            out_specs=[pl.BlockSpec((size, width // 2), lambda step, *_: (0, 0)) for size in sizes],
            scratch_shapes=[scratch, scratch],
        ),
        out_shape=[jax.ShapeDtypeStruct((size, width // 2), F32) for size in sizes],
        compiler_params=pltpu.CompilerParams(vmem_limit_bytes=VMEM_LIMIT),
        cost_estimate=pl.CostEstimate(
            flops=2 * each * 2 * 9 * padded * 512 * width // 2,
            bytes_accessed=each * (2 * half * width * 4 + 2 * shares * padded * depth * 2) + 4 * sum(sizes) * width // 2,
            transcendentals=0,
        ),
        name="project",
    )(place, wave, keep, recv, table)


def finish_kernel(place_ref, wave_ref, mine_ref, cross_ref, up_ref, down_ref, *refs, share, chunk):
    out_ref, energy_ref = refs[-2:]
    each = out_ref.shape[0]
    core = place_ref[0]
    start = (2 * place_ref[1] + core) * share
    lanes = 128
    terms = []
    spots = []
    for pair in range(each):
        first_m = wave_ref[chunk * each + pair]
        for parity in range(2):
            unit = 2 * pair + parity
            rows = slice(unit * share, (unit + 1) * share)
            value = ((mine_ref[rows, :] + cross_ref[rows, :]) + (up_ref[rows, :] + down_ref[rows, :])).T
            out_ref[pair, parity] = value.reshape(out_ref.shape[2:])
            squares = jnp.sum(value * value, axis=0, keepdims=True)
            squares = jnp.concatenate([squares, jnp.zeros((1, lanes - share), F32)], 1)
            column = lax.broadcasted_iota(jnp.int32, (1, lanes), 1)
            slot = start + column
            count = (NDEG - first_m - parity + 1) // 2
            leading = slot < count
            second_m = NDEG - 1 - first_m
            degree = jnp.where(leading, first_m + parity + 2 * slot, second_m + parity + 2 * (slot - count))
            owner_m = jnp.where(leading, first_m, second_m)
            usable = (column < share) & (degree >= 1) & (degree <= NDEG - 1)
            safe = jnp.maximum(degree, 1).astype(F32)
            factor = jnp.where(owner_m == 0, 1.0, 2.0)
            terms.append(jnp.where(usable, factor * squares / (4.0 * safe * (safe + 1.0)), 0.0))
            spots.append(jnp.where(usable, degree - 1, 0))
    term = jnp.concatenate(terms, 1)
    spot = jnp.concatenate(spots, 1)
    size = term.shape[1]
    band = lax.broadcasted_iota(jnp.int32, (16, size), 0)
    left = jnp.where(spot // lanes == band, term, 0.0)
    line = lax.broadcasted_iota(jnp.int32, (lanes, size), 0)
    right = jnp.where(spot % lanes == line, 1.0, 0.0).astype(BF16)
    first = left.astype(BF16)
    rest = left - first.astype(F32)
    second = rest.astype(BF16)
    third = (rest - second.astype(F32)).astype(BF16)
    energy_ref[...] = dot_nt(first, right) + dot_nt(second, right) + dot_nt(third, right)


def finish(place, wave, parts, held, shape, share, chunk, chunks):
    each = shape[0] // chunks
    rows, width = parts[2].shape
    full = pl.BlockSpec((rows, width), lambda step, *_: (0, 0))
    operands = list(parts)
    in_specs = [full] * 4
    aliases = {}
    if held is not None:
        operands.append(held)
        in_specs.append(pl.BlockSpec(memory_space=pl.ANY))
        aliases = {6: 0}
    return pl.pallas_call(
        functools.partial(finish_kernel, share=share, chunk=chunk),
        grid_spec=pltpu.PrefetchScalarGridSpec(
            num_scalar_prefetch=2,
            grid=(1,),
            in_specs=in_specs,
            out_specs=[
                pl.BlockSpec((each,) + shape[1:], lambda step, *_: (chunk, 0, 0, 0, 0)),
                pl.BlockSpec((16, 128), lambda step, *_: (0, 0)),
            ],
        ),
        out_shape=[jax.ShapeDtypeStruct(shape, F32), jax.ShapeDtypeStruct((16, 128), F32)],
        input_output_aliases=aliases,
        compiler_params=pltpu.CompilerParams(vmem_limit_bytes=VMEM_LIMIT),
        cost_estimate=pl.CostEstimate(
            flops=10 * 4 * rows * width, bytes_accessed=6 * rows * width * 4, transcendentals=0
        ),
        name="finish",
    )(place, wave, *operands)


def all_sum(x):
    for axis, bit in (("band", 1), ("lev", 1), ("wave", 1), ("wave", 2), ("band", 2), ("wave", 4), ("band", 4)):
        size = lax.axis_size(axis)
        x = x + lax.ppermute(x, axis, [(i, i ^ bit) for i in range(size)])
    return x


def shards(fourier, legendre, pair_m, mirror):
    bands = lax.axis_size("band")
    chips = bands // 2
    rows, pairs, members, comps, levs = fourier.shape
    half_rows = rows // 2
    slots = legendre.shape[3]
    share = slots // bands
    padded = (share + 15) // 16 * 16
    position = lax.axis_index("band")
    chip, core = position // 2, position % 2
    place = jnp.stack([core, chip, jnp.int32(chips)]).astype(jnp.int32)

    north_base = position % chips * rows
    south_base = north_base + chips * rows
    partner = lax.dynamic_slice(mirror, (north_base,), (rows,)) - south_base
    plain = (jnp.arange(rows, dtype=jnp.int32) + half_rows) % rows
    index = jnp.where(position < chips, plain, partner).reshape(rows, 1)
    send_index, keep_index = index[:half_rows], index[half_rows:]
    field = jnp.transpose(fourier, (1, 2, 3, 4, 0)).reshape(pairs, members * comps * levs, rows)

    received = []
    for chunk in range(CHUNKS):
        piece = pick_rows(place, send_index, field, chunk, CHUNKS)
        received.append(send_along(piece, chips // 2, 0))
        place, legendre, piece = lax.optimization_barrier((place, legendre, piece))

    kept = pick_rows(place, keep_index, field, 0, 1)
    table = lay_out(legendre, share, padded)

    shape = (pairs, 2, comps, levs, share)
    length = 2 * pairs // CHUNKS * share
    cut = (length // 2 + 7) // 8 * 8

    mine, cross, far = {}, {}, {}

    def part(chunk, ahead, first=0, last=length):
        at = 0 if ahead == 2 else min(ahead, 2) * length
        other = cross[chunk][0 if ahead == 2 else 1][at + first : at + last]
        return mine[chunk][ahead * length + first : ahead * length + last] + other

    def begin(chunk, after):
        mine[chunk], *others = project(place, pair_m, kept, behind(received[chunk], after), table, share, chunk)
        cross[chunk] = [send_along(other, 0, 1) for other in others]

    def send_far(chunk, after):
        cross[chunk][0] = behind(cross[chunk][0], after)
        up, down = part(chunk, 2, 0, cut), part(chunk, 2, cut, length)
        far[chunk] = (send_along(up, 1, 0), send_along(down, -1, 0))
        return up, down

    def send_near(chunk, after):
        far_up, far_down = behind(far[chunk], after)
        up = part(chunk, 1) + jnp.pad(far_up, ((0, length - cut), (0, 0)))
        down = part(chunk, 3) + jnp.pad(far_down, ((cut, 0), (0, 0)))
        far[chunk] = (send_along(up, 1, 0), send_along(down, -1, 0))
        return up, down

    begin(0, ())
    begin(1, ())
    send_far(0, ())
    begin(2, far[0])
    send_far(1, ())
    send_far(2, ())
    for chunk in range(CHUNKS):
        send_near(chunk, ())
    held = None
    energies = []
    for chunk in range(CHUNKS):
        held, energy = finish(
            place, pair_m, (mine[chunk], cross[chunk][1]) + far[chunk], held, shape, share, chunk, CHUNKS
        )
        energies.append(energy)
    total = all_sum(functools.reduce(jnp.add, energies))
    return (held, jnp.log(total.reshape(-1)[: NDEG - 1]))


def solution(mesh):
    return jax.shard_map(
        shards,
        mesh=mesh,
        in_specs=(
            P("band", "wave", None, None, "lev"),
            P("wave", "band", None, None),
            P("wave"),
            P(),
        ),
        out_specs=(P("wave", None, None, "lev", "band"), P()),
        check_vma=False,
    )
```

```python
import functools

import jax
import jax.numpy as jnp
from jax import lax
from jax.experimental import pallas as pl
from jax.experimental.pallas import tpu as pltpu
from jax.sharding import PartitionSpec as P

NDEG = 1280
MESSAGES = (2, 4, 6)
RUNS = ((0, 1), (2,))
F32 = jnp.float32
BF16 = jnp.bfloat16
VMEM_LIMIT = 48 * 1024 * 1024


def behind(x, after):
    return lax.optimization_barrier((x, after))[0]


def split_two(x):
    high = x.astype(BF16)
    low = (x - high.astype(F32)).astype(BF16)
    return high, low


def dot_nt(a, b):
    return lax.dot_general(a, b, (((1,), (1,)), ((), ())), preferred_element_type=F32)


def dot_nn(a, b):
    return jnp.dot(a, b, preferred_element_type=F32)


def send_along(x, up, cross):
    size = lax.axis_size("band")
    chips = size // 2
    pairs = [(i, ((i // 2 + up) % chips) * 2 + ((i % 2) ^ cross)) for i in range(size)]
    return lax.ppermute(x, "band", pairs)


def pick_kernel(index_ref, field_ref, send_ref, keep_ref, main_ref, tail_ref):
    count, main = main_ref.shape
    half = count // 2
    rows = field_ref.shape[2]

    @pl.when(pl.program_id(0) == 0)
    def _():
        lanes = lax.broadcasted_iota(jnp.int32, (count, rows), 1)
        chosen = jnp.where(index_ref[...] == lanes, 1.0, 0.0)
        main_ref[...] = chosen[:, :main].astype(BF16)
        tail_ref[...] = jnp.concatenate([chosen[:, main:], chosen[:, main:]], 1).astype(BF16)

    high, low = split_two(field_ref[0])
    tail = jnp.concatenate([high[:, main:], low[:, main:]], 1)
    picked = dot_nt(main_ref[...], high[:, :main]) + dot_nt(main_ref[...], low[:, :main]) + dot_nt(tail_ref[...], tail)
    send_ref[0] = picked[:half]
    keep_ref[0] = picked[half:]


def pick_rows(index, field, first, each):
    pairs, width, rows = field.shape
    count = index.shape[0]
    half = count // 2
    main = 256
    shape = jax.ShapeDtypeStruct((each, half, width), F32)
    out = pl.BlockSpec((1, half, width), lambda step: (step, 0, 0))
    return pl.pallas_call(
        pick_kernel,
        grid=(each,),
        in_specs=[
            pl.BlockSpec((count, 1), lambda step: (0, 0)),
            pl.BlockSpec((1, width, rows), lambda step: (first + step, 0, 0)),
        ],
        out_specs=[out, out],
        out_shape=[shape, shape],
        scratch_shapes=[pltpu.VMEM((count, main), BF16), pltpu.VMEM((count, 2 * (rows - main)), BF16)],
        compiler_params=pltpu.CompilerParams(vmem_limit_bytes=VMEM_LIMIT),
        cost_estimate=pl.CostEstimate(flops=10**12, bytes_accessed=10**10, transcendentals=0),
        name="pick_rows",
    )(index, field)


def layout_kernel(*refs, share):
    out_ref = refs[-1]
    lanes = main = 128
    half = refs[0].shape[1]
    rest = main - 3 * (half - main)
    for parity in range(2):
        for tile, ref in enumerate(refs[:-1]):
            high, low = split_two(ref.reshape(1, 2 * half, lanes)[0, pl.ds(parity, half, stride=2), :])
            blocks = (
                high[:main],
                low[:main],
                jnp.concatenate([high[main:], high[main:], low[main:], jnp.zeros((rest, lanes), BF16)], 0),
            )
            for i, block in enumerate(blocks):
                turned = block.T
                for s in range(out_ref.shape[2]):
                    first = max(s * share, tile * lanes)
                    last = min((s + 1) * share, (tile + 1) * lanes)
                    if first < last:
                        out_ref[0, parity, s, first - s * share : last - s * share, main * i : main * (i + 1)] = turned[
                            first - tile * lanes : last - tile * lanes
                        ]


def lay_out(table, share, padded):
    pairs, half, _, slots = table.shape
    shares = slots // share
    tiles = (slots + 127) // 128

    def block(tile):
        return pl.BlockSpec((1, half, 2, 128), lambda step: (step, 0, 0, tile))

    return pl.pallas_call(
        functools.partial(layout_kernel, share=share),
        grid=(pairs,),
        in_specs=[block(tile) for tile in range(tiles)],
        out_specs=pl.BlockSpec((1, 2, shares, padded, 384), lambda step: (step, 0, 0, 0, 0)),
        out_shape=jax.ShapeDtypeStruct((pairs, 2, shares, padded, 384), BF16),
        compiler_params=pltpu.CompilerParams(vmem_limit_bytes=VMEM_LIMIT),
        cost_estimate=pl.CostEstimate(flops=10**12, bytes_accessed=10**10, transcendentals=0),
        name="lay_out",
    )(*[table] * tiles)


def project_kernel(
    place_ref, wave_ref, *refs, share, first, ways, starts
):
    count = len(starts)
    keep_refs, recv_refs = refs[:count], refs[count : 2 * count]
    table_ref, mine_ref, *cross_refs, field_ref, result_ref = refs[2 * count :]
    step = pl.program_id(0)
    core = place_ref[0]
    chip = place_ref[1]
    chips = place_ref[2]
    first_m = wave_ref[first + step]
    half = keep_refs[0].shape[1]
    width = keep_refs[0].shape[2] // 2
    main = 128
    tail = half - main
    shares, padded = table_ref.shape[2:4]
    middle = shares // 2
    side = jnp.where(chip < chips // 2, 1.0, -1.0)
    for parity in range(2):
        keep, recv = keep_refs[0][0], recv_refs[0][0]
        for start, keep_ref, recv_ref in zip(starts[1:], keep_refs[1:], recv_refs[1:]):
            keep = jnp.where(step >= start, keep_ref[0], keep)
            recv = jnp.where(step >= start, recv_ref[0], recv)
        folded = side * (keep - recv) if parity else keep + recv
        high, low = split_two(folded)
        for member in range(2):
            part = slice(member * width, (member + 1) * width)
            field_ref[member, :main] = high[:main, part]
            field_ref[member, main : 2 * main] = low[:main, part]
            field_ref[member, 2 * main : 3 * main] = high[:main, part]
            for k, value in enumerate((high, low, high)):
                at = 3 * main + k * tail
                field_ref[member, at : at + tail] = value[main:, part]
            field_ref[member, 3 * main + 3 * tail :] = jnp.zeros((main - 3 * tail, width), BF16)
        count = (NDEG - first_m - parity + 1) // 2

        def product(member, begin, end):
            table = table_ref[0, parity, begin:end].reshape((end - begin) * padded, table_ref.shape[4])
            table = jnp.concatenate([table[:, :main], table], 1)
            result = dot_nn(table, field_ref[member])
            result_ref[member, begin:end] = result.reshape(end - begin, padded, width)

        product(0, 0, middle)
        product(1, middle, shares)
        pl.when(count > middle * share)(lambda: product(0, middle, shares))
        pl.when(count < middle * share)(lambda: product(1, middle - 1, middle))

        def store(which, rows, way):
            value = result_ref[0, which]
            if which >= middle - 1:
                slot = which * share + lax.broadcasted_iota(jnp.int32, (padded, width), 0)
                valid = parity + 2 * (slot - count) <= first_m
                value = jnp.where(slot < count, value, jnp.where(valid, result_ref[1, which], 0.0))
            value = value[:share]
            ahead = lax.rem(which // 2 + chips - chip, chips)
            back = chips // 2 + way
            toward = (1 + way) // 2
            spot = jnp.where(ahead == 0, 3, jnp.where(ahead == chips // 2, toward, jnp.where(ahead == back, 2, 1 - toward)))
            mine = core == which % 2

            @pl.when(mine)
            def _():
                mine_ref[spot, rows, :] = value

            base = 0
            for cross_ref in cross_refs:
                size = cross_ref.shape[0]

                @pl.when(jnp.logical_not(mine) & (spot >= base) & (spot < base + size))
                def _():
                    cross_ref[jnp.clip(spot - base, 0, size - 1), rows, :] = value

                base += size

        for pair, (way, at) in enumerate(ways):

            @pl.when(step == pair)
            def _():
                for which in range(shares):
                    begin = at + parity * share
                    store(which, slice(begin, begin + share), way)


def project(place, wave, keeps, recvs, table, share, first, ways, rows, messages):
    half, width = recvs[0].shape[1:]
    shares, padded, depth = table.shape[2:]
    sizes_in = [recv.shape[0] for recv in recvs]
    starts = [sum(sizes_in[:i]) for i in range(len(recvs))]

    def field(start, size):
        return pl.BlockSpec((1, half, width), lambda step, *_: (jnp.clip(step - start, 0, size - 1), 0, 0))

    fields = [field(start, size) for start, size in zip(starts, sizes_in)]
    sizes = [(count, rows, width // 2) for count in (shares // 2, *messages)]
    return pl.pallas_call(
        functools.partial(project_kernel, share=share, first=first, ways=ways, starts=starts),
        grid_spec=pltpu.PrefetchScalarGridSpec(
            num_scalar_prefetch=2,
            grid=(len(ways),),
            in_specs=[
                *fields,
                *fields,
                pl.BlockSpec((1,) + table.shape[1:], lambda step, *_: (first + step, 0, 0, 0, 0)),
            ],
            out_specs=[pl.BlockSpec(size, lambda step, *_: (0, 0, 0)) for size in sizes],
            scratch_shapes=[
                pltpu.VMEM((2, 512, width // 2), BF16),
                pltpu.VMEM((2, shares, padded, width // 2), F32),
            ],
        ),
        out_shape=[jax.ShapeDtypeStruct(size, F32) for size in sizes],
        compiler_params=pltpu.CompilerParams(vmem_limit_bytes=VMEM_LIMIT),
        cost_estimate=pl.CostEstimate(flops=10**12, bytes_accessed=10**10, transcendentals=0),
        name="project",
    )(place, wave, *keeps, *recvs, table)


def finish_kernel(place_ref, wave_ref, mine_ref, cross_ref, far_up_ref, far_down_ref, near_up_ref, near_down_ref, *refs, share, first, ways
):
    out_ref, energy_ref = refs[-2:]
    low = far_up_ref.shape[0]
    each = out_ref.shape[0]
    core = place_ref[0]
    start = (2 * place_ref[1] + core) * share
    lanes = 128
    terms = []
    spots = []
    for pair in range(each):
        first_m = wave_ref[first + pair]
        for parity in range(2):
            at = ways[pair][1] + parity * share
            rows = slice(at, at + share)
            if at < low:
                arrived = far_up_ref[rows, :] + near_down_ref[rows, :]
            else:
                arrived = far_down_ref[at - low : at - low + share, :] + near_up_ref[rows, :]
            value = ((mine_ref[0, rows, :] + cross_ref[0, rows, :]) + arrived).T
            out_ref[pair, parity] = value.reshape(out_ref.shape[2:])
            squares = jnp.sum(value * value, axis=0, keepdims=True)
            squares = jnp.concatenate([squares, jnp.zeros((1, lanes - share), F32)], 1)
            column = lax.broadcasted_iota(jnp.int32, (1, lanes), 1)
            slot = start + column
            count = (NDEG - first_m - parity + 1) // 2
            leading = slot < count
            second_m = NDEG - 1 - first_m
            degree = jnp.where(leading, first_m + parity + 2 * slot, second_m + parity + 2 * (slot - count))
            owner_m = jnp.where(leading, first_m, second_m)
            usable = (column < share) & (degree >= 1) & (degree <= NDEG - 1)
            safe = jnp.maximum(degree, 1).astype(F32)
            factor = jnp.where(owner_m == 0, 1.0, 2.0)
            terms.append(jnp.where(usable, factor * squares / (4.0 * safe * (safe + 1.0)), 0.0))
            spots.append(jnp.where(usable, degree - 1, 0))
    term = jnp.concatenate(terms, 1)
    spot = jnp.concatenate(spots, 1)
    size = term.shape[1]
    band = lax.broadcasted_iota(jnp.int32, (16, size), 0)
    left = jnp.where(spot // lanes == band, term, 0.0)
    line = lax.broadcasted_iota(jnp.int32, (lanes, size), 0)
    right = jnp.where(spot % lanes == line, 1.0, 0.0).astype(BF16)
    first = left.astype(BF16)
    rest = left - first.astype(F32)
    second = rest.astype(BF16)
    third = (rest - second.astype(F32)).astype(BF16)
    energy_ref[...] = dot_nt(first, right) + dot_nt(second, right) + dot_nt(third, right)


def finish(place, wave, mine, cross, far, near, held, shape, share, first, ways):
    each = len(ways)
    _, rows, width = mine.shape
    messages = far + near
    operands = [mine, cross] + messages
    in_specs = [
        pl.BlockSpec((1, rows, width), lambda step, *_: (3, 0, 0)),
        pl.BlockSpec((1, rows, width), lambda step, *_: (cross.shape[0] - 1, 0, 0)),
    ] + [pl.BlockSpec(message.shape, lambda step, *_: (0, 0)) for message in messages]
    aliases = {}
    if held is not None:
        operands.append(held)
        in_specs.append(pl.BlockSpec(memory_space=pl.ANY))
        aliases = {1 + len(operands): 0}
    return pl.pallas_call(
        functools.partial(finish_kernel, share=share, first=first, ways=ways),
        grid_spec=pltpu.PrefetchScalarGridSpec(
            num_scalar_prefetch=2,
            grid=(1,),
            in_specs=in_specs,
            out_specs=[
                pl.BlockSpec((each,) + shape[1:], lambda step, *_: (first // each, 0, 0, 0, 0)),
                pl.BlockSpec((16, 128), lambda step, *_: (0, 0)),
            ],
        ),
        out_shape=[jax.ShapeDtypeStruct(shape, F32), jax.ShapeDtypeStruct((16, 128), F32)],
        input_output_aliases=aliases,
        compiler_params=pltpu.CompilerParams(vmem_limit_bytes=VMEM_LIMIT),
        cost_estimate=pl.CostEstimate(flops=10**12, bytes_accessed=10**10, transcendentals=0),
        name="finish",
    )(place, wave, *operands)


def all_sum(x):
    for axis, bit in (("band", 1), ("lev", 1), ("wave", 1), ("wave", 2), ("band", 2), ("wave", 4), ("band", 4)):
        size = lax.axis_size(axis)
        x = x + lax.ppermute(x, axis, [(i, i ^ bit) for i in range(size)])
    return x


def shards(fourier, legendre, pair_m, mirror):
    bands = lax.axis_size("band")
    chips = bands // 2
    rows, pairs, members, comps, levs = fourier.shape
    half_rows = rows // 2
    slots = legendre.shape[3]
    share = slots // bands
    padded = (share + 15) // 16 * 16
    position = lax.axis_index("band")
    chip, core = position // 2, position % 2
    place = jnp.stack([core, chip, jnp.int32(chips)]).astype(jnp.int32)

    north_base = position % chips * rows
    south_base = north_base + chips * rows
    partner = lax.dynamic_slice(mirror, (north_base,), (rows,)) - south_base
    plain = (jnp.arange(rows, dtype=jnp.int32) + half_rows) % rows
    index = jnp.where(position < chips, plain, partner).reshape(rows, 1)
    field = jnp.transpose(fourier, (1, 2, 3, 4, 0)).reshape(pairs, members * comps * levs, rows)

    kept, received = [], []
    for i, each in enumerate(MESSAGES):
        message, keep = pick_rows(index, field, sum(MESSAGES[:i]), each)
        kept.append(keep)
        received.append(send_along(message, chips // 2, 0))
        index, legendre, message = lax.optimization_barrier((index, legendre, message))

    table = lay_out(legendre, share, padded)

    ways, lengths, firsts = [], [], []
    for run in RUNS:
        each = sum(MESSAGES[i] for i in run)
        ups = (each + len(ways)) // 2
        low = (2 * ups * share + 7) // 8 * 8
        high = (2 * (each - ups) * share + 7) // 8 * 8
        firsts.append(sum(MESSAGES[: run[0]]))
        ways.append([(-1, 2 * i * share) if i < ups else (1, low + 2 * (i - ups) * share) for i in range(each)])
        lengths.append((low, high))
    mine, cross, far, near = {}, {}, {}, {}

    def begin(run, messages, after):
        mine[run], *others = project(
            place, pair_m, [kept[i] for i in RUNS[run]], behind([received[i] for i in RUNS[run]], after), table, share,
            firsts[run], ways[run], sum(lengths[run]), messages,
        )
        cross[run] = [send_along(other, 0, 1) for other in others]

    def other_core(run, spot):
        for message in cross[run]:
            if spot < message.shape[0]:
                return message[spot]
            spot -= message.shape[0]

    def send_early(run, after):
        totals = [mine[run][spot] + other for spot, other in enumerate(behind([other_core(run, 0), other_core(run, 1)], after))]
        near[run] = [send_along(totals[0], 1, 0), send_along(totals[1], -1, 0)]
        return totals

    def send_late(run):
        low, _ = lengths[run]
        total, other = mine[run][2], other_core(run, 2)
        totals = [
            total[:low] + other[:low] + near[run][0][:low],
            total[low:] + other[low:] + near[run][1][low:],
        ]
        far[run] = [send_along(totals[0], 1, 0), send_along(totals[1], -1, 0)]
        return totals

    begin(0, (1, 1, 1, 1), ())
    begin(1, (1, 1, 2), [send_early(0, ()), cross[0][2:]])
    sent = send_late(0)
    send_early(1, sent)
    send_late(1)
    shape = (pairs, 2, comps, levs, share)
    held = None
    energies = []
    for run in range(len(RUNS)):
        held, energy = finish(
            place, pair_m, mine[run], cross[run][-1], far[run], near[run], held, shape, share, firsts[run], ways[run]
        )
        energies.append(energy)
    total = all_sum(functools.reduce(jnp.add, energies))
    return (held, jnp.log(total.reshape(-1)[: NDEG - 1]))


def solution(mesh):
    return jax.shard_map(
        shards,
        mesh=mesh,
        in_specs=(
            P("band", "wave", None, None, "lev"),
            P("wave", "band", None, None),
            P("wave"),
            P(),
        ),
        out_specs=(P("wave", None, None, "lev", "band"), P()),
        check_vma=False,
    )
```

```python
import functools

import jax
import jax.numpy as jnp
from jax import lax
from jax.experimental import pallas as pl
from jax.experimental.pallas import tpu as pltpu
from jax.sharding import PartitionSpec as P

NDEG = 1280
MESSAGES = (2, 4, 6)
RUNS = ((0, 1), (2,))
F32 = jnp.float32
BF16 = jnp.bfloat16
VMEM_LIMIT = 48 * 1024 * 1024
VMEM_SMALL = 16 * 1024 * 1024


def behind(x, after):
    return lax.optimization_barrier((x, after))[0]


def split_two(x):
    high = x.astype(BF16)
    low = (x - high.astype(F32)).astype(BF16)
    return high, low


def split_three(x):
    high = x.astype(BF16)
    rest = x - high.astype(F32)
    middle = rest.astype(BF16)
    return high, middle, (rest - middle.astype(F32)).astype(BF16)


def dot_nt(a, b):
    return lax.dot_general(a, b, (((1,), (1,)), ((), ())), preferred_element_type=F32)


def dot_nn(a, b):
    return jnp.dot(a, b, preferred_element_type=F32)


def send_along(x, up, cross):
    size = lax.axis_size("band")
    chips = size // 2
    pairs = [(i, ((i // 2 + up) % chips) * 2 + ((i % 2) ^ cross)) for i in range(size)]
    return lax.ppermute(x, "band", pairs)


def pick_kernel(index_ref, field_ref, send_ref, keep_ref, main_ref, tail_ref):
    count, main = main_ref.shape
    half = count // 2
    rows = field_ref.shape[2]

    @pl.when(pl.program_id(0) == 0)
    def _():
        lanes = lax.broadcasted_iota(jnp.int32, (count, rows), 1)
        chosen = jnp.where(index_ref[...] == lanes, 1.0, 0.0)
        main_ref[...] = chosen[:, :main].astype(BF16)
        tail_ref[...] = jnp.concatenate([chosen[:, main:], chosen[:, main:]], 1).astype(BF16)

    high, low = split_two(field_ref[0])
    tail = jnp.concatenate([high[:, main:], low[:, main:]], 1)
    picked = dot_nt(main_ref[...], high[:, :main]) + dot_nt(main_ref[...], low[:, :main]) + dot_nt(tail_ref[...], tail)
    send_ref[0] = picked[:half]
    keep_ref[0] = picked[half:]


def pick_rows(index, field, first, each):
    pairs, width, rows = field.shape
    count = index.shape[0]
    half = count // 2
    main = 256
    shape = jax.ShapeDtypeStruct((each, half, width), F32)
    out = pl.BlockSpec((1, half, width), lambda step: (step, 0, 0))
    return pl.pallas_call(
        pick_kernel,
        grid=(each,),
        in_specs=[
            pl.BlockSpec((count, 1), lambda step: (0, 0)),
            pl.BlockSpec((1, width, rows), lambda step: (first + step, 0, 0)),
        ],
        out_specs=[out, out],
        out_shape=[shape, shape],
        scratch_shapes=[pltpu.VMEM((count, main), BF16), pltpu.VMEM((count, 2 * (rows - main)), BF16)],
        compiler_params=pltpu.CompilerParams(vmem_limit_bytes=VMEM_LIMIT),
        cost_estimate=pl.CostEstimate(flops=10**12, bytes_accessed=10**10, transcendentals=0),
        name="pick_rows",
    )(index, field)


def layout_kernel(*refs, share):
    out_ref = refs[-1]
    lanes = main = 128
    half = refs[0].shape[1]
    rest = main - 3 * (half - main)
    for parity in range(2):
        for tile, ref in enumerate(refs[:-1]):
            high, low = split_two(ref.reshape(1, 2 * half, lanes)[0, pl.ds(parity, half, stride=2), :])
            blocks = (
                high[:main],
                low[:main],
                jnp.concatenate([high[main:], high[main:], low[main:], jnp.zeros((rest, lanes), BF16)], 0),
            )
            for i, block in enumerate(blocks):
                turned = block.T
                for s in range(out_ref.shape[2]):
                    first = max(s * share, tile * lanes)
                    last = min((s + 1) * share, (tile + 1) * lanes)
                    if first < last:
                        out_ref[0, parity, s, first - s * share : last - s * share, main * i : main * (i + 1)] = turned[
                            first - tile * lanes : last - tile * lanes
                        ]


def lay_out(table, share, padded):
    pairs, half, _, slots = table.shape
    shares = slots // share
    tiles = (slots + 127) // 128

    def block(tile):
        return pl.BlockSpec((1, half, 2, 128), lambda step: (step, 0, 0, tile))

    return pl.pallas_call(
        functools.partial(layout_kernel, share=share),
        grid=(pairs,),
        in_specs=[block(tile) for tile in range(tiles)],
        out_specs=pl.BlockSpec((1, 2, shares, padded, 384), lambda step: (step, 0, 0, 0, 0)),
        out_shape=jax.ShapeDtypeStruct((pairs, 2, shares, padded, 384), BF16),
        compiler_params=pltpu.CompilerParams(vmem_limit_bytes=VMEM_LIMIT),
        cost_estimate=pl.CostEstimate(flops=10**12, bytes_accessed=10**10, transcendentals=0),
        name="lay_out",
    )(*[table] * tiles)


def owner_of(place, step, ups, chip, chips):
    up = jnp.where(step < ups, 1, 0)
    ahead = (1 + up, 2 + up, jnp.where(step < ups, 1, chips - 1), 0)[place]
    return lax.rem(chip + ahead, chips)


def project_kernel(place_ref, wave_ref, *refs, share, first, starts, ups):
    count = len(starts)
    keep_refs, recv_refs = refs[:count], refs[count : 2 * count]
    table_ref, mine_ref, *cross_refs, field_ref, result_ref = refs[2 * count :]
    step = pl.program_id(0)
    core = place_ref[0]
    chip = place_ref[1]
    chips = place_ref[2]
    first_m = wave_ref[first + step]
    half = keep_refs[0].shape[1]
    width = keep_refs[0].shape[2] // 2
    main = 128
    tail = half - main
    shares, padded = table_ref.shape[2:4]
    middle = shares // 2
    side = jnp.where(chip < chips // 2, 1.0, -1.0)
    for parity in range(2):
        keep, recv = keep_refs[0][0], recv_refs[0][0]
        for start, keep_ref, recv_ref in zip(starts[1:], keep_refs[1:], recv_refs[1:]):
            keep = jnp.where(step >= start, keep_ref[0], keep)
            recv = jnp.where(step >= start, recv_ref[0], recv)
        folded = side * (keep - recv) if parity else keep + recv
        high, low = split_two(folded)
        for member in range(2):
            part = slice(member * width, (member + 1) * width)
            field_ref[member, :main] = high[:main, part]
            field_ref[member, main : 2 * main] = low[:main, part]
            field_ref[member, 2 * main : 3 * main] = high[:main, part]
            for k, value in enumerate((high, low, high)):
                at = 3 * main + k * tail
                field_ref[member, at : at + tail] = value[main:, part]
            field_ref[member, 3 * main + 3 * tail :] = jnp.zeros((main - 3 * tail, width), BF16)
        count = lax.shift_right_logical(NDEG - first_m - parity + 1, 1)

        def product(member, begin, end):
            table = table_ref[0, parity, begin:end].reshape((end - begin) * padded, table_ref.shape[4])
            table = jnp.concatenate([table[:, :main], table], 1)
            result_ref[member, begin:end] = dot_nn(table, field_ref[member]).reshape(end - begin, padded, width)

        product(0, 0, middle)
        product(1, middle, shares)
        pl.when(count > middle * share)(lambda: product(0, middle, shares))
        pl.when(count < middle * share)(lambda: product(1, middle - 1, middle))

        for local in range(ups):

            @pl.when(lax.rem(step, ups) == local)
            def _():
                begin = (2 * local + parity) * share
                rows = slice(begin, begin + share)
                outs = [mine_ref.at[spot] for spot in range(4)] + [ref.at[i] for ref in cross_refs for i in range(ref.shape[0])]
                for i, out_ref in enumerate(outs):
                    which = 2 * owner_of(i % 4, step, ups, chip, chips) + (core if i < 4 else 1 - core)
                    slot = which * share + lax.broadcasted_iota(jnp.int32, (padded, width), 0)
                    valid = parity + 2 * (slot - count) <= first_m
                    value = jnp.where(slot < count, result_ref[0, which], jnp.where(valid, result_ref[1, which], 0.0))
                    out_ref[rows, :] = value[:share]


def project(place, wave, keeps, recvs, table, share, first, messages):
    half, width = recvs[0].shape[1:]
    shares, padded, depth = table.shape[2:]
    sizes = [recv.shape[0] for recv in recvs]
    starts = [sum(sizes[:i]) for i in range(len(recvs))]
    ups = sum(sizes) // 2
    rows = run_rows(ups, share)

    def field(start, size):
        return pl.BlockSpec((1, half, width), lambda step, *_: (jnp.clip(step - start, 0, size - 1), 0, 0))

    fields = [field(start, size) for start, size in zip(starts, sizes)]
    counts = (shares // 2, *messages)
    return pl.pallas_call(
        functools.partial(project_kernel, share=share, first=first, starts=starts, ups=ups),
        grid_spec=pltpu.PrefetchScalarGridSpec(
            num_scalar_prefetch=2,
            grid=(2 * ups,),
            in_specs=[
                *fields,
                *fields,
                pl.BlockSpec((1,) + table.shape[1:], lambda step, *_: (first + step, 0, 0, 0, 0)),
            ],
            out_specs=[pl.BlockSpec((count, rows, width // 2), lambda step, *_: (0, step // ups, 0)) for count in counts],
            scratch_shapes=[
                pltpu.VMEM((2, 512, width // 2), BF16),
                pltpu.VMEM((2, shares, padded, width // 2), F32),
            ],
        ),
        out_shape=[jax.ShapeDtypeStruct((count, 2 * rows, width // 2), F32) for count in counts],
        compiler_params=pltpu.CompilerParams(vmem_limit_bytes=VMEM_LIMIT),
        cost_estimate=pl.CostEstimate(flops=10**12, bytes_accessed=10**10, transcendentals=0),
        name="project",
    )(place, wave, *keeps, *recvs, table)


def run_rows(ups, share):
    return (2 * ups * share + 7) // 8 * 8


def energy_kernel(
    place_ref, wave_ref, mine_ref, cross_ref, far_up_ref, far_down_ref, near_up_ref, near_down_ref, so_far_ref, out_ref,
    *, share, first, ways,
):
    low = far_up_ref.shape[0]
    lanes = out_ref.shape[1]
    halves = []
    for rows, far_ref, near_ref in (
        (slice(None, low), far_up_ref, near_down_ref),
        (slice(low, None), far_down_ref, near_up_ref),
    ):
        value = (mine_ref[0, rows, :] + cross_ref[0, rows, :]) + (far_ref[...] + near_ref[rows, :])
        squares = value * value
        halves.append(squares[:, :lanes] + squares[:, lanes:])
    squares = jnp.concatenate(halves, 0)
    ones = jnp.ones((8, lanes), BF16)
    squares = sum(dot_nt(ones, piece) for piece in split_three(squares))[:1]

    size = squares.shape[1]
    column = lax.broadcasted_iota(jnp.int32, (1, size), 1)
    start = (2 * place_ref[1] + place_ref[0]) * share
    first_m = jnp.zeros((1, size), jnp.int32)
    parity = jnp.zeros((1, size), jnp.int32)
    slot = jnp.full((1, size), -1, jnp.int32)
    for pair, at in enumerate(ways):
        for s in range(2):
            begin = at + s * share
            inside = (column >= begin) & (column < begin + share)
            first_m = jnp.where(inside, wave_ref[first + pair], first_m)
            parity = jnp.where(inside, s, parity)
            slot = jnp.where(inside, column - begin + start, slot)
    count = lax.shift_right_logical(NDEG - first_m - parity + 1, 1)
    leading = slot < count
    second_m = NDEG - 1 - first_m
    degree = jnp.where(leading, first_m + parity + 2 * slot, second_m + parity + 2 * (slot - count))
    owner_m = jnp.where(leading, first_m, second_m)
    usable = (slot >= 0) & (degree >= 1) & (degree <= NDEG - 1)
    safe = jnp.maximum(degree, 1).astype(F32)
    factor = jnp.where(owner_m == 0, 1.0, 2.0)
    term = jnp.where(usable, factor * squares / (4.0 * safe * (safe + 1.0)), 0.0)
    spot = jnp.where(usable, degree - 1, 0)
    band = lax.broadcasted_iota(jnp.int32, (out_ref.shape[0], size), 0)
    left = jnp.where(lax.shift_right_logical(spot, 7) == band, term, 0.0)
    line = lax.broadcasted_iota(jnp.int32, (lanes, size), 0)
    right = jnp.where((spot & (lanes - 1)) == line, 1.0, 0.0).astype(BF16)
    out_ref[...] = so_far_ref[...] + sum(dot_nt(piece, right) for piece in split_three(left))


def run_energy(place, wave, parts, so_far, share, first, ways):
    _, rows, width = parts[0].shape
    return pl.pallas_call(
        functools.partial(energy_kernel, share=share, first=first, ways=ways),
        grid_spec=pltpu.PrefetchScalarGridSpec(
            num_scalar_prefetch=2,
            grid=(1,),
            in_specs=own_parts(parts) + [pl.BlockSpec(so_far.shape, lambda step, *_: (0, 0))],
            out_specs=pl.BlockSpec(so_far.shape, lambda step, *_: (0, 0)),
        ),
        out_shape=jax.ShapeDtypeStruct(so_far.shape, F32),
        compiler_params=pltpu.CompilerParams(vmem_limit_bytes=VMEM_SMALL),
        cost_estimate=pl.CostEstimate(flops=10 * rows * width, bytes_accessed=4 * rows * width * 4, transcendentals=0),
        name="run_energy",
    )(place, wave, *parts, so_far)


def own_parts(parts):
    _, rows, width = parts[0].shape
    return [
        pl.BlockSpec((1, rows, width), lambda step, *_: (parts[0].shape[0] - 1, 0, 0)),
        pl.BlockSpec((1, rows, width), lambda step, *_: (parts[1].shape[0] - 1, 0, 0)),
    ] + [pl.BlockSpec(part.shape, lambda step, *_: (0, 0)) for part in parts[2:]]


def place_kernel(mine_ref, cross_ref, far_up_ref, far_down_ref, near_up_ref, near_down_ref, *refs, share, ways):
    out_ref = refs[-1]
    low = far_up_ref.shape[0]
    for pair, at in enumerate(ways):
        for parity in range(2):
            begin = at + parity * share
            rows = slice(begin, begin + share)
            if begin < low:
                arrived = far_up_ref[rows, :] + near_down_ref[rows, :]
            else:
                arrived = far_down_ref[begin - low : begin - low + share, :] + near_up_ref[rows, :]
            value = ((mine_ref[0, rows, :] + cross_ref[0, rows, :]) + arrived).T
            out_ref[pair, parity] = value.reshape(out_ref.shape[2:])


def place_run(parts, held, shape, share, first, ways):
    each = len(ways)
    _, rows, width = parts[0].shape
    return pl.pallas_call(
        functools.partial(place_kernel, share=share, ways=ways),
        grid=(1,),
        in_specs=own_parts(parts) + [pl.BlockSpec(memory_space=pl.ANY)] * len(held),
        out_specs=pl.BlockSpec((each,) + shape[1:], lambda step: (first // each, 0, 0, 0, 0)),
        out_shape=jax.ShapeDtypeStruct(shape, F32),
        input_output_aliases={len(parts): 0} if held else {},
        compiler_params=pltpu.CompilerParams(vmem_limit_bytes=VMEM_SMALL),
        cost_estimate=pl.CostEstimate(flops=4 * rows * width, bytes_accessed=5 * rows * width * 4, transcendentals=0),
        name="place_run",
    )(*parts, *held)


def all_sum(x):
    for axis, bit in (("band", 1), ("band", 2), ("band", 4), ("wave", 1), ("lev", 1), ("wave", 2), ("wave", 4)):
        size = lax.axis_size(axis)
        x = x + lax.ppermute(x, axis, [(i, i ^ bit) for i in range(size)])
    return x


def shards(fourier, legendre, pair_m, mirror):
    bands = lax.axis_size("band")
    chips = bands // 2
    rows, pairs, members, comps, levs = fourier.shape
    half_rows = rows // 2
    slots = legendre.shape[3]
    share = slots // bands
    padded = (share + 15) // 16 * 16
    position = lax.axis_index("band")
    chip, core = position // 2, position % 2
    place = jnp.stack([core, chip, jnp.int32(chips)]).astype(jnp.int32)

    north_base = position % chips * rows
    south_base = north_base + chips * rows
    partner = lax.dynamic_slice(mirror, (north_base,), (rows,)) - south_base
    plain = (jnp.arange(rows, dtype=jnp.int32) + half_rows) % rows
    index = jnp.where(position < chips, plain, partner).reshape(rows, 1)
    field = jnp.transpose(fourier, (1, 2, 3, 4, 0)).reshape(pairs, members * comps * levs, rows)

    kept, received = [], []
    for i, each in enumerate(MESSAGES):
        message, keep = pick_rows(index, field, sum(MESSAGES[:i]), each)
        kept.append(keep)
        received.append(send_along(message, chips // 2, 0))
        index, legendre, message = lax.optimization_barrier((index, legendre, message))

    table = lay_out(legendre, share, padded)

    firsts = [sum(MESSAGES[: run[0]]) for run in RUNS]
    ways = []
    mine, cross, near, far = {}, {}, {}, {}
    for run in RUNS:
        ups = sum(MESSAGES[i] for i in run) // 2
        ways.append([half * run_rows(ups, share) + 2 * i * share for half in range(2) for i in range(ups)])

    def begin(run, messages, after):
        mine[run], *others = project(
            place, pair_m, [kept[i] for i in RUNS[run]], behind([received[i] for i in RUNS[run]], after), table, share,
            firsts[run], messages,
        )
        cross[run] = [send_along(other, 0, 1) for other in others]

    def send_early(run, after):
        totals = [mine[run][spot] + other[0] for spot, other in enumerate(behind(cross[run][:2], after))]
        near[run] = [send_along(totals[0], 1, 0), send_along(totals[1], -1, 0)]
        return totals

    def send_late(run):
        total, other = mine[run][2], cross[run][2][0]
        low = total.shape[0] // 2
        totals = [
            total[:low] + other[:low] + near[run][0][:low],
            total[low:] + other[low:] + near[run][1][low:],
        ]
        far[run] = [send_along(totals[0], 1, 0), send_along(totals[1], -1, 0)]
        return totals

    begin(0, (1, 1, 1, 1), ())
    begin(1, (1, 1, 2), [send_early(0, ()), cross[0][2:]])
    send_early(1, near[0])
    send_late(0)
    send_late(1)
    shape = (pairs, 2, comps, levs, share)
    held = []
    total = jnp.zeros((16, 128), F32)
    for run in range(len(RUNS)):
        parts = [mine[run], cross[run][-1]] + far[run] + near[run]
        total = run_energy(place, pair_m, parts, behind(total, held), share, firsts[run], ways[run])
        held = [place_run(parts, held, shape, share, firsts[run], ways[run])]
    total = all_sum(total)
    return (held[0], jnp.log(total.reshape(-1)[: NDEG - 1]))


def solution(mesh):
    return jax.shard_map(
        shards,
        mesh=mesh,
        in_specs=(
            P("band", "wave", None, None, "lev"),
            P("wave", "band", None, None),
            P("wave"),
            P(),
        ),
        out_specs=(P("wave", None, None, "lev", "band"), P()),
        check_vma=False,
    )
```

```python
import functools

import jax
import jax.numpy as jnp
from jax import lax
from jax.experimental import pallas as pl
from jax.experimental.pallas import tpu as pltpu
from jax.sharding import PartitionSpec as P

NDEG = 1280
MESSAGES = (1, 2, 3, 6)
RUNS = ((0, 1, 2), (3,))
F32 = jnp.float32
BF16 = jnp.bfloat16
VMEM_LIMIT = 48 * 1024 * 1024
VMEM_SMALL = 16 * 1024 * 1024


def behind(x, after):
    return lax.optimization_barrier((x, after))[0]


def split_two(x):
    high = x.astype(BF16)
    low = (x - high.astype(F32)).astype(BF16)
    return high, low


def split_three(x):
    high = x.astype(BF16)
    rest = x - high.astype(F32)
    middle = rest.astype(BF16)
    return high, middle, (rest - middle.astype(F32)).astype(BF16)


def dot_nt(a, b):
    return lax.dot_general(a, b, (((1,), (1,)), ((), ())), preferred_element_type=F32)


def dot_nn(a, b):
    return jnp.dot(a, b, preferred_element_type=F32)


def send_along(x, up, cross):
    size = lax.axis_size("band")
    chips = size // 2
    pairs = [(i, ((i // 2 + up) % chips) * 2 + ((i % 2) ^ cross)) for i in range(size)]
    return lax.ppermute(x, "band", pairs)


def pick_kernel(index_ref, field_ref, send_ref, keep_ref, main_ref, tail_ref):
    count, main = main_ref.shape
    half = count // 2
    rows = field_ref.shape[2]

    @pl.when(pl.program_id(0) == 0)
    def _():
        lanes = lax.broadcasted_iota(jnp.int32, (count, rows), 1)
        chosen = jnp.where(index_ref[...] == lanes, 1.0, 0.0)
        main_ref[...] = chosen[:, :main].astype(BF16)
        tail_ref[...] = jnp.concatenate([chosen[:, main:], chosen[:, main:]], 1).astype(BF16)

    high, low = split_two(field_ref[0])
    tail = jnp.concatenate([high[:, main:], low[:, main:]], 1)
    picked = dot_nt(main_ref[...], high[:, :main]) + dot_nt(main_ref[...], low[:, :main]) + dot_nt(tail_ref[...], tail)
    send_ref[0] = picked[:half]
    keep_ref[0] = picked[half:]


def pick_rows(index, field, first, each):
    pairs, width, rows = field.shape
    count = index.shape[0]
    half = count // 2
    main = 256
    shape = jax.ShapeDtypeStruct((each, half, width), F32)
    out = pl.BlockSpec((1, half, width), lambda step: (step, 0, 0))
    return pl.pallas_call(
        pick_kernel,
        grid=(each,),
        in_specs=[
            pl.BlockSpec((count, 1), lambda step: (0, 0)),
            pl.BlockSpec((1, width, rows), lambda step: (first + step, 0, 0)),
        ],
        out_specs=[out, out],
        out_shape=[shape, shape],
        scratch_shapes=[pltpu.VMEM((count, main), BF16), pltpu.VMEM((count, 2 * (rows - main)), BF16)],
        compiler_params=pltpu.CompilerParams(vmem_limit_bytes=VMEM_LIMIT),
        cost_estimate=pl.CostEstimate(flops=10**12, bytes_accessed=10**10, transcendentals=0),
        name="pick_rows",
    )(index, field)


def layout_kernel(*refs, share):
    out_ref = refs[-1]
    lanes = main = 128
    half = refs[0].shape[1]
    rest = main - 3 * (half - main)
    for parity in range(2):
        for tile, ref in enumerate(refs[:-1]):
            high, low = split_two(ref.reshape(1, 2 * half, lanes)[0, pl.ds(parity, half, stride=2), :])
            blocks = (
                high[:main],
                low[:main],
                jnp.concatenate([high[main:], high[main:], low[main:], jnp.zeros((rest, lanes), BF16)], 0),
            )
            for i, block in enumerate(blocks):
                turned = block.T
                for s in range(out_ref.shape[2]):
                    first = max(s * share, tile * lanes)
                    last = min((s + 1) * share, (tile + 1) * lanes)
                    if first < last:
                        out_ref[0, parity, s, first - s * share : last - s * share, main * i : main * (i + 1)] = turned[
                            first - tile * lanes : last - tile * lanes
                        ]


def lay_out(table, share, padded):
    pairs, half, _, slots = table.shape
    shares = slots // share
    tiles = (slots + 127) // 128

    def block(tile):
        return pl.BlockSpec((1, half, 2, 128), lambda step: (step, 0, 0, tile))

    return pl.pallas_call(
        functools.partial(layout_kernel, share=share),
        grid=(pairs,),
        in_specs=[block(tile) for tile in range(tiles)],
        out_specs=pl.BlockSpec((1, 2, shares, padded, 384), lambda step: (step, 0, 0, 0, 0)),
        out_shape=jax.ShapeDtypeStruct((pairs, 2, shares, padded, 384), BF16),
        compiler_params=pltpu.CompilerParams(vmem_limit_bytes=VMEM_LIMIT),
        cost_estimate=pl.CostEstimate(flops=10**12, bytes_accessed=10**10, transcendentals=0),
        name="lay_out",
    )(*[table] * tiles)


def owner_of(place, step, ups, chip, chips):
    up = jnp.where(step < ups, 1, 0)
    ahead = (1 + up, 2 + up, jnp.where(step < ups, 1, chips - 1), 0)[place]
    return lax.rem(chip + ahead, chips)


def project_kernel(place_ref, wave_ref, *refs, share, first, starts, ups):
    count = len(starts)
    keep_refs, recv_refs = refs[:count], refs[count : 2 * count]
    table_ref, mine_ref, *cross_refs, field_ref, result_ref = refs[2 * count :]
    step = pl.program_id(0)
    core = place_ref[0]
    chip = place_ref[1]
    chips = place_ref[2]
    first_m = wave_ref[first + step]
    half = keep_refs[0].shape[1]
    width = keep_refs[0].shape[2] // 2
    main = 128
    tail = half - main
    shares, padded = table_ref.shape[2:4]
    middle = shares // 2
    side = jnp.where(chip < chips // 2, 1.0, -1.0)
    for parity in range(2):
        keep, recv = keep_refs[0][0], recv_refs[0][0]
        for start, keep_ref, recv_ref in zip(starts[1:], keep_refs[1:], recv_refs[1:]):
            keep = jnp.where(step >= start, keep_ref[0], keep)
            recv = jnp.where(step >= start, recv_ref[0], recv)
        folded = side * (keep - recv) if parity else keep + recv
        high, low = split_two(folded)
        for member in range(2):
            part = slice(member * width, (member + 1) * width)
            field_ref[member, :main] = high[:main, part]
            field_ref[member, main : 2 * main] = low[:main, part]
            field_ref[member, 2 * main : 3 * main] = high[:main, part]
            for k, value in enumerate((high, low, high)):
                at = 3 * main + k * tail
                field_ref[member, at : at + tail] = value[main:, part]
            field_ref[member, 3 * main + 3 * tail :] = jnp.zeros((main - 3 * tail, width), BF16)
        count = lax.shift_right_logical(NDEG - first_m - parity + 1, 1)

        def product(member, begin, end):
            table = table_ref[0, parity, begin:end].reshape((end - begin) * padded, table_ref.shape[4])
            table = jnp.concatenate([table[:, :main], table], 1)
            result_ref[member, begin:end] = dot_nn(table, field_ref[member]).reshape(end - begin, padded, width)

        product(0, 0, middle)
        product(1, middle, shares)
        pl.when(count > middle * share)(lambda: product(0, middle, shares))
        pl.when(count < middle * share)(lambda: product(1, middle - 1, middle))

        for local in range(ups):

            @pl.when(lax.rem(step, ups) == local)
            def _():
                begin = (2 * local + parity) * share
                rows = slice(begin, begin + share)
                outs = [mine_ref.at[spot] for spot in range(4)] + [ref.at[i] for ref in cross_refs for i in range(ref.shape[0])]
                for i, out_ref in enumerate(outs):
                    which = 2 * owner_of(i % 4, step, ups, chip, chips) + (core if i < 4 else 1 - core)
                    slot = which * share + lax.broadcasted_iota(jnp.int32, (padded, width), 0)
                    valid = parity + 2 * (slot - count) <= first_m
                    value = jnp.where(slot < count, result_ref[0, which], jnp.where(valid, result_ref[1, which], 0.0))
                    out_ref[rows, :] = value[:share]


def project(place, wave, keeps, recvs, table, share, first, messages):
    half, width = recvs[0].shape[1:]
    shares, padded, depth = table.shape[2:]
    sizes = [recv.shape[0] for recv in recvs]
    starts = [sum(sizes[:i]) for i in range(len(recvs))]
    ups = sum(sizes) // 2
    rows = run_rows(ups, share)

    def field(start, size):
        return pl.BlockSpec((1, half, width), lambda step, *_: (jnp.clip(step - start, 0, size - 1), 0, 0))

    fields = [field(start, size) for start, size in zip(starts, sizes)]
    counts = (shares // 2, *messages)
    return pl.pallas_call(
        functools.partial(project_kernel, share=share, first=first, starts=starts, ups=ups),
        grid_spec=pltpu.PrefetchScalarGridSpec(
            num_scalar_prefetch=2,
            grid=(2 * ups,),
            in_specs=[
                *fields,
                *fields,
                pl.BlockSpec((1,) + table.shape[1:], lambda step, *_: (first + step, 0, 0, 0, 0)),
            ],
            out_specs=[pl.BlockSpec((count, rows, width // 2), lambda step, *_: (0, step // ups, 0)) for count in counts],
            scratch_shapes=[
                pltpu.VMEM((2, 512, width // 2), BF16),
                pltpu.VMEM((2, shares, padded, width // 2), F32),
            ],
        ),
        out_shape=[jax.ShapeDtypeStruct((count, 2 * rows, width // 2), F32) for count in counts],
        compiler_params=pltpu.CompilerParams(vmem_limit_bytes=40 * 1024 * 1024),
        cost_estimate=pl.CostEstimate(flops=10**12, bytes_accessed=10**10, transcendentals=0),
        name="project",
    )(place, wave, *keeps, *recvs, table)


def run_rows(ups, share):
    return (2 * ups * share + 7) // 8 * 8


def energy_kernel(
    place_ref, wave_ref, mine_ref, cross_ref, far_up_ref, far_down_ref, near_up_ref, near_down_ref, so_far_ref, out_ref,
    *, share, first, ways,
):
    low = far_up_ref.shape[0]
    lanes = out_ref.shape[1]
    halves = []
    for rows, far_ref, near_ref in (
        (slice(None, low), far_up_ref, near_down_ref),
        (slice(low, None), far_down_ref, near_up_ref),
    ):
        value = (mine_ref[0, rows, :] + cross_ref[0, rows, :]) + (far_ref[...] + near_ref[rows, :])
        squares = value * value
        halves.append(squares[:, :lanes] + squares[:, lanes:])
    squares = jnp.concatenate(halves, 0)
    ones = jnp.ones((8, lanes), BF16)
    squares = sum(dot_nt(ones, piece) for piece in split_three(squares))[:1]

    size = squares.shape[1]
    column = lax.broadcasted_iota(jnp.int32, (1, size), 1)
    start = (2 * place_ref[1] + place_ref[0]) * share
    first_m = jnp.zeros((1, size), jnp.int32)
    parity = jnp.zeros((1, size), jnp.int32)
    slot = jnp.full((1, size), -1, jnp.int32)
    for pair, at in enumerate(ways):
        for s in range(2):
            begin = at + s * share
            inside = (column >= begin) & (column < begin + share)
            first_m = jnp.where(inside, wave_ref[first + pair], first_m)
            parity = jnp.where(inside, s, parity)
            slot = jnp.where(inside, column - begin + start, slot)
    count = lax.shift_right_logical(NDEG - first_m - parity + 1, 1)
    leading = slot < count
    second_m = NDEG - 1 - first_m
    degree = jnp.where(leading, first_m + parity + 2 * slot, second_m + parity + 2 * (slot - count))
    owner_m = jnp.where(leading, first_m, second_m)
    usable = (slot >= 0) & (degree >= 1) & (degree <= NDEG - 1)
    safe = jnp.maximum(degree, 1).astype(F32)
    factor = jnp.where(owner_m == 0, 1.0, 2.0)
    term = jnp.where(usable, factor * squares / (4.0 * safe * (safe + 1.0)), 0.0)
    spot = jnp.where(usable, degree - 1, 0)
    band = lax.broadcasted_iota(jnp.int32, (out_ref.shape[0], size), 0)
    left = jnp.where(lax.shift_right_logical(spot, 7) == band, term, 0.0)
    line = lax.broadcasted_iota(jnp.int32, (lanes, size), 0)
    right = jnp.where((spot & (lanes - 1)) == line, 1.0, 0.0).astype(BF16)
    out_ref[...] = so_far_ref[...] + sum(dot_nt(piece, right) for piece in split_three(left))


def run_energy(place, wave, parts, so_far, share, first, ways):
    _, rows, width = parts[0].shape
    return pl.pallas_call(
        functools.partial(energy_kernel, share=share, first=first, ways=ways),
        grid_spec=pltpu.PrefetchScalarGridSpec(
            num_scalar_prefetch=2,
            grid=(1,),
            in_specs=own_parts(parts) + [pl.BlockSpec(so_far.shape, lambda step, *_: (0, 0))],
            out_specs=pl.BlockSpec(so_far.shape, lambda step, *_: (0, 0)),
        ),
        out_shape=jax.ShapeDtypeStruct(so_far.shape, F32),
        compiler_params=pltpu.CompilerParams(vmem_limit_bytes=VMEM_SMALL),
        cost_estimate=pl.CostEstimate(flops=10 * rows * width, bytes_accessed=4 * rows * width * 4, transcendentals=0),
        name="run_energy",
    )(place, wave, *parts, so_far)


def own_parts(parts):
    _, rows, width = parts[0].shape
    return [
        pl.BlockSpec((1, rows, width), lambda step, *_: (parts[0].shape[0] - 1, 0, 0)),
        pl.BlockSpec((1, rows, width), lambda step, *_: (parts[1].shape[0] - 1, 0, 0)),
    ] + [pl.BlockSpec(part.shape, lambda step, *_: (0, 0)) for part in parts[2:]]


def place_kernel(mine_ref, cross_ref, far_up_ref, far_down_ref, near_up_ref, near_down_ref, *refs, share, ways):
    out_ref = refs[-1]
    low = far_up_ref.shape[0]
    for pair, at in enumerate(ways):
        for parity in range(2):
            begin = at + parity * share
            rows = slice(begin, begin + share)
            if begin < low:
                arrived = far_up_ref[rows, :] + near_down_ref[rows, :]
            else:
                arrived = far_down_ref[begin - low : begin - low + share, :] + near_up_ref[rows, :]
            value = ((mine_ref[0, rows, :] + cross_ref[0, rows, :]) + arrived).T
            out_ref[pair, parity] = value.reshape(out_ref.shape[2:])


def place_run(parts, held, shape, share, first, ways):
    each = len(ways)
    _, rows, width = parts[0].shape
    return pl.pallas_call(
        functools.partial(place_kernel, share=share, ways=ways),
        grid=(1,),
        in_specs=own_parts(parts) + [pl.BlockSpec(memory_space=pl.ANY)] * len(held),
        out_specs=pl.BlockSpec((each,) + shape[1:], lambda step: (first // each, 0, 0, 0, 0)),
        out_shape=jax.ShapeDtypeStruct(shape, F32),
        input_output_aliases={len(parts): 0} if held else {},
        compiler_params=pltpu.CompilerParams(vmem_limit_bytes=VMEM_SMALL),
        cost_estimate=pl.CostEstimate(flops=4 * rows * width, bytes_accessed=5 * rows * width * 4, transcendentals=0),
        name="place_run",
    )(*parts, *held)


def all_sum(x):
    for axis, bit in (("band", 1), ("band", 2), ("band", 4), ("wave", 1), ("lev", 1), ("wave", 2), ("wave", 4)):
        size = lax.axis_size(axis)
        x = x + lax.ppermute(x, axis, [(i, i ^ bit) for i in range(size)])
    return x


def shards(fourier, legendre, pair_m, mirror):
    bands = lax.axis_size("band")
    chips = bands // 2
    rows, pairs, members, comps, levs = fourier.shape
    half_rows = rows // 2
    slots = legendre.shape[3]
    share = slots // bands
    padded = (share + 15) // 16 * 16
    position = lax.axis_index("band")
    chip, core = position // 2, position % 2
    place = jnp.stack([core, chip, jnp.int32(chips)]).astype(jnp.int32)

    north_base = position % chips * rows
    south_base = north_base + chips * rows
    partner = lax.dynamic_slice(mirror, (north_base,), (rows,)) - south_base
    plain = (jnp.arange(rows, dtype=jnp.int32) + half_rows) % rows
    index = jnp.where(position < chips, plain, partner).reshape(rows, 1)
    field = jnp.transpose(fourier, (1, 2, 3, 4, 0)).reshape(pairs, members * comps * levs, rows)

    kept, received = [], []
    for i, each in enumerate(MESSAGES):
        message, keep = pick_rows(index, field, sum(MESSAGES[:i]), each)
        kept.append(keep)
        received.append(send_along(message, chips // 2, 0))
        index, legendre, message = lax.optimization_barrier((index, legendre, message))

    table = lay_out(legendre, share, padded)

    firsts = [sum(MESSAGES[: run[0]]) for run in RUNS]
    ways = []
    mine, cross, near, far = {}, {}, {}, {}
    for run in RUNS:
        ups = sum(MESSAGES[i] for i in run) // 2
        ways.append([half * run_rows(ups, share) + 2 * i * share for half in range(2) for i in range(ups)])

    def begin(run, messages, after):
        mine[run], *others = project(
            place, pair_m, [kept[i] for i in RUNS[run]], behind([received[i] for i in RUNS[run]], after), table, share,
            firsts[run], messages,
        )
        cross[run] = [send_along(other, 0, 1) for other in others]

    def send_early(run, after):
        totals = [mine[run][spot] + other[0] for spot, other in enumerate(behind(cross[run][:2], after))]
        near[run] = [send_along(totals[0], 1, 0), send_along(totals[1], -1, 0)]
        return totals

    def send_late(run):
        total, other = mine[run][2], cross[run][2][0]
        low = total.shape[0] // 2
        totals = [
            total[:low] + other[:low] + near[run][0][:low],
            total[low:] + other[low:] + near[run][1][low:],
        ]
        far[run] = [send_along(totals[0], 1, 0), send_along(totals[1], -1, 0)]
        return totals

    begin(0, (1, 1, 1, 1), ())
    begin(1, (1, 1, 2), [send_early(0, ()), cross[0][2:]])
    send_early(1, near[0])
    send_late(0)
    send_late(1)
    shape = (pairs, 2, comps, levs, share)
    held = []
    total = jnp.zeros((16, 128), F32)
    for run in range(len(RUNS)):
        parts = [mine[run], cross[run][-1]] + far[run] + near[run]
        total = run_energy(place, pair_m, parts, behind(total, held), share, firsts[run], ways[run])
        held = [place_run(parts, held, shape, share, firsts[run], ways[run])]
    total = all_sum(total)
    return (held[0], jnp.log(total.reshape(-1)[: NDEG - 1]))


def solution(mesh):
    return jax.shard_map(
        shards,
        mesh=mesh,
        in_specs=(
            P("band", "wave", None, None, "lev"),
            P("wave", "band", None, None),
            P("wave"),
            P(),
        ),
        out_specs=(P("wave", None, None, "lev", "band"), P()),
        check_vma=False,
    )
```

```python
import functools

import jax
import jax.numpy as jnp
from jax import lax
from jax.experimental import pallas as pl
from jax.experimental.pallas import tpu as pltpu
from jax.sharding import PartitionSpec as P

NDEG = 1280
MESSAGES = (1, 2, 3, 6)
RUNS = ((0, 1, 2), (3,))
F32 = jnp.float32
BF16 = jnp.bfloat16
VMEM_LIMIT = 48 * 1024 * 1024
VMEM_SMALL = 16 * 1024 * 1024


def behind(x, after):
    return lax.optimization_barrier((x, after))[0]


def split_two(x):
    high = x.astype(BF16)
    low = (x - high.astype(F32)).astype(BF16)
    return high, low


def split_three(x):
    high = x.astype(BF16)
    rest = x - high.astype(F32)
    middle = rest.astype(BF16)
    return high, middle, (rest - middle.astype(F32)).astype(BF16)


def dot_nt(a, b):
    return lax.dot_general(a, b, (((1,), (1,)), ((), ())), preferred_element_type=F32)


def dot_nn(a, b):
    return jnp.dot(a, b, preferred_element_type=F32)


def send_along(x, up, cross):
    size = lax.axis_size("band")
    chips = size // 2
    pairs = [(i, ((i // 2 + up) % chips) * 2 + ((i % 2) ^ cross)) for i in range(size)]
    return lax.ppermute(x, "band", pairs)


def pick_kernel(index_ref, field_ref, send_ref, keep_ref, main_ref, tail_ref):
    count, main = main_ref.shape
    half = count // 2
    rows = field_ref.shape[2]

    @pl.when(pl.program_id(0) == 0)
    def _():
        lanes = lax.broadcasted_iota(jnp.int32, (count, rows), 1)
        chosen = jnp.where(index_ref[...] == lanes, 1.0, 0.0)
        main_ref[...] = chosen[:, :main].astype(BF16)
        tail_ref[...] = jnp.concatenate([chosen[:, main:], chosen[:, main:]], 1).astype(BF16)

    high, low = split_two(field_ref[0])
    tail = jnp.concatenate([high[:, main:], low[:, main:]], 1)
    picked = dot_nt(main_ref[...], high[:, :main]) + dot_nt(main_ref[...], low[:, :main]) + dot_nt(tail_ref[...], tail)
    send_ref[0] = picked[:half]
    keep_ref[0] = picked[half:]


def pick_rows(index, field, first, each):
    pairs, width, rows = field.shape
    count = index.shape[0]
    half = count // 2
    main = 256
    shape = jax.ShapeDtypeStruct((each, half, width), F32)
    out = pl.BlockSpec((1, half, width), lambda step: (step, 0, 0))
    return pl.pallas_call(
        pick_kernel,
        grid=(each,),
        in_specs=[
            pl.BlockSpec((count, 1), lambda step: (0, 0)),
            pl.BlockSpec((1, width, rows), lambda step: (first + step, 0, 0)),
        ],
        out_specs=[out, out],
        out_shape=[shape, shape],
        scratch_shapes=[pltpu.VMEM((count, main), BF16), pltpu.VMEM((count, 2 * (rows - main)), BF16)],
        compiler_params=pltpu.CompilerParams(vmem_limit_bytes=VMEM_LIMIT),
        cost_estimate=pl.CostEstimate(flops=10**12, bytes_accessed=10**10, transcendentals=0),
        name="pick_rows",
    )(index, field)


def layout_kernel(*refs, share):
    out_ref = refs[-1]
    lanes = main = 128
    half = refs[0].shape[1]
    rest = main - 3 * (half - main)
    for parity in range(2):
        for tile, ref in enumerate(refs[:-1]):
            high, low = split_two(ref.reshape(1, 2 * half, lanes)[0, pl.ds(parity, half, stride=2), :])
            blocks = (
                high[:main],
                low[:main],
                jnp.concatenate([high[main:], high[main:], low[main:], jnp.zeros((rest, lanes), BF16)], 0),
            )
            for i, block in enumerate(blocks):
                turned = block.T
                for s in range(out_ref.shape[2]):
                    first = max(s * share, tile * lanes)
                    last = min((s + 1) * share, (tile + 1) * lanes)
                    if first < last:
                        out_ref[0, parity, s, first - s * share : last - s * share, main * i : main * (i + 1)] = turned[
                            first - tile * lanes : last - tile * lanes
                        ]


def lay_out(table, share, padded):
    pairs, half, _, slots = table.shape
    shares = slots // share
    tiles = (slots + 127) // 128

    def block(tile):
        return pl.BlockSpec((1, half, 2, 128), lambda step: (step, 0, 0, tile))

    return pl.pallas_call(
        functools.partial(layout_kernel, share=share),
        grid=(pairs,),
        in_specs=[block(tile) for tile in range(tiles)],
        out_specs=pl.BlockSpec((1, 2, shares, padded, 384), lambda step: (step, 0, 0, 0, 0)),
        out_shape=jax.ShapeDtypeStruct((pairs, 2, shares, padded, 384), BF16),
        compiler_params=pltpu.CompilerParams(vmem_limit_bytes=VMEM_LIMIT),
        cost_estimate=pl.CostEstimate(flops=10**12, bytes_accessed=10**10, transcendentals=0),
        name="lay_out",
    )(*[table] * tiles)


def owner_of(place, step, ups, chip, chips):
    up = jnp.where(step < ups, 1, 0)
    ahead = (1 + up, 2 + up, jnp.where(step < ups, 1, chips - 1), 0)[place]
    return lax.rem(chip + ahead, chips)


def project_kernel(place_ref, wave_ref, *refs, share, first, starts, ups):
    count = len(starts)
    keep_refs, recv_refs = refs[:count], refs[count : 2 * count]
    table_ref, mine_ref, *cross_refs, field_ref, result_ref = refs[2 * count :]
    step = pl.program_id(0)
    core = place_ref[0]
    chip = place_ref[1]
    chips = place_ref[2]
    first_m = wave_ref[first + step]
    half = keep_refs[0].shape[1]
    width = keep_refs[0].shape[2] // 2
    main = 128
    tail = half - main
    shares, padded = table_ref.shape[2:4]
    middle = shares // 2
    side = jnp.where(chip < chips // 2, 1.0, -1.0)
    for parity in range(2):
        keep, recv = keep_refs[0][0], recv_refs[0][0]
        for start, keep_ref, recv_ref in zip(starts[1:], keep_refs[1:], recv_refs[1:]):
            keep = jnp.where(step >= start, keep_ref[0], keep)
            recv = jnp.where(step >= start, recv_ref[0], recv)
        folded = side * (keep - recv) if parity else keep + recv
        high, low = split_two(folded)
        for member in range(2):
            part = slice(member * width, (member + 1) * width)
            field_ref[member, :main] = high[:main, part]
            field_ref[member, main : 2 * main] = low[:main, part]
            field_ref[member, 2 * main : 3 * main] = high[:main, part]
            for k, value in enumerate((high, low, high)):
                at = 3 * main + k * tail
                field_ref[member, at : at + tail] = value[main:, part]
            field_ref[member, 3 * main + 3 * tail :] = jnp.zeros((main - 3 * tail, width), BF16)
        count = lax.shift_right_logical(NDEG - first_m - parity + 1, 1)

        def product(member, begin, end):
            table = table_ref[0, parity, begin:end].reshape((end - begin) * padded, table_ref.shape[4])
            table = jnp.concatenate([table[:, :main], table], 1)
            result_ref[member, begin:end] = dot_nn(table, field_ref[member]).reshape(end - begin, padded, width)

        product(0, 0, middle)
        product(1, middle, shares)
        pl.when(count > middle * share)(lambda: product(0, middle, shares))
        pl.when(count < middle * share)(lambda: product(1, middle - 1, middle))

        for local in range(ups):

            @pl.when(lax.rem(step, ups) == local)
            def _():
                begin = (2 * local + parity) * share
                rows = slice(begin, begin + share)
                outs = [mine_ref.at[spot] for spot in range(4)] + [ref.at[i] for ref in cross_refs for i in range(ref.shape[0])]
                for i, out_ref in enumerate(outs):
                    which = 2 * owner_of(i % 4, step, ups, chip, chips) + (core if i < 4 else 1 - core)
                    slot = which * share + lax.broadcasted_iota(jnp.int32, (padded, width), 0)
                    valid = parity + 2 * (slot - count) <= first_m
                    value = jnp.where(slot < count, result_ref[0, which], jnp.where(valid, result_ref[1, which], 0.0))
                    out_ref[rows, :] = value[:share]


def project(place, wave, keeps, recvs, table, share, first, messages):
    half, width = recvs[0].shape[1:]
    shares, padded, depth = table.shape[2:]
    sizes = [recv.shape[0] for recv in recvs]
    starts = [sum(sizes[:i]) for i in range(len(recvs))]
    ups = sum(sizes) // 2
    rows = run_rows(ups, share)

    def field(start, size):
        return pl.BlockSpec((1, half, width), lambda step, *_: (jnp.clip(step - start, 0, size - 1), 0, 0))

    fields = [field(start, size) for start, size in zip(starts, sizes)]
    counts = (shares // 2, *messages)
    return pl.pallas_call(
        functools.partial(project_kernel, share=share, first=first, starts=starts, ups=ups),
        grid_spec=pltpu.PrefetchScalarGridSpec(
            num_scalar_prefetch=2,
            grid=(2 * ups,),
            in_specs=[
                *fields,
                *fields,
                pl.BlockSpec((1,) + table.shape[1:], lambda step, *_: (first + step, 0, 0, 0, 0)),
            ],
            out_specs=[pl.BlockSpec((count, rows, width // 2), lambda step, *_: (0, step // ups, 0)) for count in counts],
            scratch_shapes=[
                pltpu.VMEM((2, 512, width // 2), BF16),
                pltpu.VMEM((2, shares, padded, width // 2), F32),
            ],
        ),
        out_shape=[jax.ShapeDtypeStruct((count, 2 * rows, width // 2), F32) for count in counts],
        compiler_params=pltpu.CompilerParams(vmem_limit_bytes=40 * 1024 * 1024),
        cost_estimate=pl.CostEstimate(flops=10**12, bytes_accessed=10**10, transcendentals=0),
        name="project",
    )(place, wave, *keeps, *recvs, table)


def run_rows(ups, share):
    return (2 * ups * share + 7) // 8 * 8


def energy_kernel(
    place_ref, wave_ref, low_ref, high_ref, far_up_ref, far_down_ref, so_far_ref, out_ref, *, share, first, ways
):
    lanes = out_ref.shape[1]
    halves = []
    for held_ref, far_ref in ((low_ref, far_up_ref), (high_ref, far_down_ref)):
        value = held_ref[...] + far_ref[...]
        squares = value * value
        halves.append(squares[:, :lanes] + squares[:, lanes:])
    squares = jnp.concatenate(halves, 0)
    ones = jnp.ones((8, lanes), BF16)
    squares = sum(dot_nt(ones, piece) for piece in split_three(squares))[:1]

    size = squares.shape[1]
    column = lax.broadcasted_iota(jnp.int32, (1, size), 1)
    start = (2 * place_ref[1] + place_ref[0]) * share
    first_m = jnp.zeros((1, size), jnp.int32)
    parity = jnp.zeros((1, size), jnp.int32)
    slot = jnp.full((1, size), -1, jnp.int32)
    for pair, at in enumerate(ways):
        for s in range(2):
            begin = at + s * share
            inside = (column >= begin) & (column < begin + share)
            first_m = jnp.where(inside, wave_ref[first + pair], first_m)
            parity = jnp.where(inside, s, parity)
            slot = jnp.where(inside, column - begin + start, slot)
    count = lax.shift_right_logical(NDEG - first_m - parity + 1, 1)
    leading = slot < count
    second_m = NDEG - 1 - first_m
    degree = jnp.where(leading, first_m + parity + 2 * slot, second_m + parity + 2 * (slot - count))
    owner_m = jnp.where(leading, first_m, second_m)
    usable = (slot >= 0) & (degree >= 1) & (degree <= NDEG - 1)
    safe = jnp.maximum(degree, 1).astype(F32)
    factor = jnp.where(owner_m == 0, 1.0, 2.0)
    term = jnp.where(usable, factor * squares / (4.0 * safe * (safe + 1.0)), 0.0)
    spot = jnp.where(usable, degree - 1, 0)
    band = lax.broadcasted_iota(jnp.int32, (out_ref.shape[0], size), 0)
    left = jnp.where(lax.shift_right_logical(spot, 7) == band, term, 0.0)
    line = lax.broadcasted_iota(jnp.int32, (lanes, size), 0)
    right = jnp.where((spot & (lanes - 1)) == line, 1.0, 0.0).astype(BF16)
    out_ref[...] = so_far_ref[...] + sum(dot_nt(piece, right) for piece in split_three(left))


def run_energy(place, wave, parts, so_far, share, first, ways):
    rows, width = parts[0].shape
    return pl.pallas_call(
        functools.partial(energy_kernel, share=share, first=first, ways=ways),
        grid_spec=pltpu.PrefetchScalarGridSpec(
            num_scalar_prefetch=2,
            grid=(1,),
            in_specs=own_parts(parts) + [pl.BlockSpec(so_far.shape, lambda step, *_: (0, 0))],
            out_specs=pl.BlockSpec(so_far.shape, lambda step, *_: (0, 0)),
        ),
        out_shape=jax.ShapeDtypeStruct(so_far.shape, F32),
        compiler_params=pltpu.CompilerParams(vmem_limit_bytes=VMEM_SMALL),
        cost_estimate=pl.CostEstimate(flops=10 * rows * width, bytes_accessed=4 * rows * width * 4, transcendentals=0),
        name="run_energy",
    )(place, wave, *parts, so_far)


def own_parts(parts):
    return [pl.BlockSpec(part.shape, lambda step, *_: (0, 0)) for part in parts]


def place_kernel(low_ref, high_ref, far_up_ref, far_down_ref, *refs, share, ways):
    out_ref = refs[-1]
    low = low_ref.shape[0]
    for pair, at in enumerate(ways):
        for parity in range(2):
            begin = at + parity * share
            held_ref, far_ref = (low_ref, far_up_ref) if begin < low else (high_ref, far_down_ref)
            rows = slice(begin % low, begin % low + share)
            value = (held_ref[rows, :] + far_ref[rows, :]).T
            out_ref[pair, parity] = value.reshape(out_ref.shape[2:])


def place_run(parts, held, shape, share, first, ways):
    each = len(ways)
    rows, width = parts[0].shape
    return pl.pallas_call(
        functools.partial(place_kernel, share=share, ways=ways),
        grid=(1,),
        in_specs=own_parts(parts) + [pl.BlockSpec(memory_space=pl.ANY)] * len(held),
        out_specs=pl.BlockSpec((each,) + shape[1:], lambda step: (first // each, 0, 0, 0, 0)),
        out_shape=jax.ShapeDtypeStruct(shape, F32),
        input_output_aliases={len(parts): 0} if held else {},
        compiler_params=pltpu.CompilerParams(vmem_limit_bytes=VMEM_SMALL),
        cost_estimate=pl.CostEstimate(flops=4 * rows * width, bytes_accessed=5 * rows * width * 4, transcendentals=0),
        name="place_run",
    )(*parts, *held)


def all_sum(x):
    for axis, bit in (("band", 1), ("band", 2), ("band", 4), ("wave", 1), ("lev", 1), ("wave", 2), ("wave", 4)):
        size = lax.axis_size(axis)
        x = x + lax.ppermute(x, axis, [(i, i ^ bit) for i in range(size)])
    return x


def shards(fourier, legendre, pair_m, mirror):
    bands = lax.axis_size("band")
    chips = bands // 2
    rows, pairs, members, comps, levs = fourier.shape
    half_rows = rows // 2
    slots = legendre.shape[3]
    share = slots // bands
    padded = (share + 15) // 16 * 16
    position = lax.axis_index("band")
    chip, core = position // 2, position % 2
    place = jnp.stack([core, chip, jnp.int32(chips)]).astype(jnp.int32)

    north_base = position % chips * rows
    south_base = north_base + chips * rows
    partner = lax.dynamic_slice(mirror, (north_base,), (rows,)) - south_base
    plain = (jnp.arange(rows, dtype=jnp.int32) + half_rows) % rows
    index = jnp.where(position < chips, plain, partner).reshape(rows, 1)
    field = jnp.transpose(fourier, (1, 2, 3, 4, 0)).reshape(pairs, members * comps * levs, rows)

    kept, received = [], []
    for i, each in enumerate(MESSAGES):
        message, keep = pick_rows(index, field, sum(MESSAGES[:i]), each)
        kept.append(keep)
        received.append(send_along(message, chips // 2, 0))
        index, legendre, message = lax.optimization_barrier((index, legendre, message))

    table = lay_out(legendre, share, padded)

    firsts = [sum(MESSAGES[: run[0]]) for run in RUNS]
    ways = []
    mine, cross, near, far = {}, {}, {}, {}
    for run in RUNS:
        ups = sum(MESSAGES[i] for i in run) // 2
        ways.append([half * run_rows(ups, share) + 2 * i * share for half in range(2) for i in range(ups)])

    def begin(run, messages, after):
        mine[run], *others = project(
            place, pair_m, [kept[i] for i in RUNS[run]], behind([received[i] for i in RUNS[run]], after), table, share,
            firsts[run], messages,
        )
        cross[run] = [send_along(other, 0, 1) for other in others]

    def send_early(run, after):
        totals = [mine[run][spot] + other[0] for spot, other in enumerate(behind(cross[run][:2], after))]
        near[run] = [send_along(totals[0], 1, 0), send_along(totals[1], -1, 0)]
        return totals

    def send_late(run):
        total, other = mine[run][2], cross[run][2][0]
        low = total.shape[0] // 2
        totals = [
            total[:low] + other[:low] + near[run][0][:low],
            total[low:] + other[low:] + near[run][1][low:],
        ]
        far[run] = [send_along(totals[0], 1, 0), send_along(totals[1], -1, 0)]
        return totals

    begin(0, (1, 1, 1, 1), ())
    begin(1, (1, 1, 2), [send_early(0, ()), cross[0][2:]])
    send_early(1, near[0])
    send_late(0)
    send_late(1)
    shape = (pairs, 2, comps, levs, share)
    held = []
    total = jnp.zeros((16, 128), F32)
    for run in range(len(RUNS)):
        own, other = mine[run][3], cross[run][-1][-1]
        low = own.shape[0] // 2
        parts = [
            own[:low] + other[:low] + near[run][1][:low],
            own[low:] + other[low:] + near[run][0][low:],
            *far[run],
        ]
        total = run_energy(place, pair_m, parts, behind(total, held), share, firsts[run], ways[run])
        held = [place_run(parts, held, shape, share, firsts[run], ways[run])]
    total = all_sum(total)
    return (held[0], jnp.log(total.reshape(-1)[: NDEG - 1]))


def solution(mesh):
    return jax.shard_map(
        shards,
        mesh=mesh,
        in_specs=(
            P("band", "wave", None, None, "lev"),
            P("wave", "band", None, None),
            P("wave"),
            P(),
        ),
        out_specs=(P("wave", None, None, "lev", "band"), P()),
        check_vma=False,
    )
```

```python
import functools

import jax
import jax.numpy as jnp
from jax import lax
from jax.experimental import pallas as pl
from jax.experimental.pallas import tpu as pltpu
from jax.sharding import PartitionSpec as P

NDEG = 1280
MESSAGES = (1, 2, 3, 6)
RUNS = ((0, 1, 2), (3,))
F32 = jnp.float32
BF16 = jnp.bfloat16
VMEM_LIMIT = 52 * 1024 * 1024
VMEM_SMALL = 32 * 1024 * 1024


def behind(x, after):
    return lax.optimization_barrier((x, after))[0]


def split_two(x):
    high = x.astype(BF16)
    low = (x - high.astype(F32)).astype(BF16)
    return high, low


def split_three(x):
    high = x.astype(BF16)
    rest = x - high.astype(F32)
    middle = rest.astype(BF16)
    return high, middle, (rest - middle.astype(F32)).astype(BF16)


def dot_nt(a, b):
    return lax.dot_general(a, b, (((1,), (1,)), ((), ())), preferred_element_type=F32)


def dot_nn(a, b):
    return jnp.dot(a, b, preferred_element_type=F32)


def send_along(x, up, cross):
    size = lax.axis_size("band")
    chips = size // 2
    pairs = [(i, ((i // 2 + up) % chips) * 2 + ((i % 2) ^ cross)) for i in range(size)]
    return lax.ppermute(x, "band", pairs)


def pick_kernel(index_ref, field_ref, send_ref, keep_ref, main_ref, tail_ref):
    count, main = main_ref.shape
    half = count // 2
    rows = field_ref.shape[2]

    @pl.when(pl.program_id(0) == 0)
    def _():
        lanes = lax.broadcasted_iota(jnp.int32, (count, rows), 1)
        chosen = jnp.where(index_ref[...] == lanes, 1.0, 0.0)
        main_ref[...] = chosen[:, :main].astype(BF16)
        tail_ref[...] = jnp.concatenate([chosen[:, main:], chosen[:, main:]], 1).astype(BF16)

    high, low = split_two(field_ref[0])
    tail = jnp.concatenate([high[:, main:], low[:, main:]], 1)
    picked = dot_nt(main_ref[...], high[:, :main]) + dot_nt(main_ref[...], low[:, :main]) + dot_nt(tail_ref[...], tail)
    send_ref[0] = picked[:half]
    keep_ref[0] = picked[half:]


def pick_rows(index, field, first, each):
    pairs, width, rows = field.shape
    count = index.shape[0]
    half = count // 2
    main = 256
    shape = jax.ShapeDtypeStruct((each, half, width), F32)
    out = pl.BlockSpec((1, half, width), lambda step: (step, 0, 0))
    return pl.pallas_call(
        pick_kernel,
        grid=(each,),
        in_specs=[
            pl.BlockSpec((count, 1), lambda step: (0, 0)),
            pl.BlockSpec((1, width, rows), lambda step: (first + step, 0, 0)),
        ],
        out_specs=[out, out],
        out_shape=[shape, shape],
        scratch_shapes=[pltpu.VMEM((count, main), BF16), pltpu.VMEM((count, 2 * (rows - main)), BF16)],
        compiler_params=pltpu.CompilerParams(vmem_limit_bytes=VMEM_LIMIT),
        cost_estimate=pl.CostEstimate(flops=10**12, bytes_accessed=10**10, transcendentals=0),
        name="pick_rows",
    )(index, field)


def layout_kernel(*refs, share):
    out_ref = refs[-1]
    lanes = main = 128
    half = refs[0].shape[1]
    rest = main - 3 * (half - main)
    for parity in range(2):
        for tile, ref in enumerate(refs[:-1]):
            high, low = split_two(ref.reshape(1, 2 * half, lanes)[0, pl.ds(parity, half, stride=2), :])
            blocks = (
                high[:main],
                low[:main],
                jnp.concatenate([high[main:], high[main:], low[main:], jnp.zeros((rest, lanes), BF16)], 0),
            )
            for i, block in enumerate(blocks):
                turned = block.T
                for s in range(out_ref.shape[2]):
                    first = max(s * share, tile * lanes)
                    last = min((s + 1) * share, (tile + 1) * lanes)
                    if first < last:
                        out_ref[0, parity, s, first - s * share : last - s * share, main * i : main * (i + 1)] = turned[
                            first - tile * lanes : last - tile * lanes
                        ]


def lay_out(table, share, padded):
    pairs, half, _, slots = table.shape
    shares = slots // share
    tiles = (slots + 127) // 128

    def block(tile):
        return pl.BlockSpec((1, half, 2, 128), lambda step: (step, 0, 0, tile))

    return pl.pallas_call(
        functools.partial(layout_kernel, share=share),
        grid=(pairs,),
        in_specs=[block(tile) for tile in range(tiles)],
        out_specs=pl.BlockSpec((1, 2, shares, padded, 384), lambda step: (step, 0, 0, 0, 0)),
        out_shape=jax.ShapeDtypeStruct((pairs, 2, shares, padded, 384), BF16),
        compiler_params=pltpu.CompilerParams(vmem_limit_bytes=VMEM_LIMIT),
        cost_estimate=pl.CostEstimate(flops=10**12, bytes_accessed=10**10, transcendentals=0),
        name="lay_out",
    )(*[table] * tiles)


def owner_of(place, step, ups, chip, chips):
    up = jnp.where(step < ups, 1, 0)
    ahead = (1 + up, 2 + up, jnp.where(step < ups, 1, chips - 1), 0)[place]
    return lax.rem(chip + ahead, chips)


def project_kernel(place_ref, wave_ref, *refs, share, first, starts, ups):
    count = len(starts)
    keep_refs, recv_refs = refs[:count], refs[count : 2 * count]
    table_ref, mine_ref, *cross_refs, field_ref, result_ref = refs[2 * count :]
    step = pl.program_id(0)
    core = place_ref[0]
    chip = place_ref[1]
    chips = place_ref[2]
    first_m = wave_ref[first + step]
    half = keep_refs[0].shape[1]
    width = keep_refs[0].shape[2] // 2
    main = 128
    tail = half - main
    shares, padded = table_ref.shape[2:4]
    middle = shares // 2
    side = jnp.where(chip < chips // 2, 1.0, -1.0)
    for parity in range(2):
        keep, recv = keep_refs[0][0], recv_refs[0][0]
        for start, keep_ref, recv_ref in zip(starts[1:], keep_refs[1:], recv_refs[1:]):
            keep = jnp.where(step >= start, keep_ref[0], keep)
            recv = jnp.where(step >= start, recv_ref[0], recv)
        folded = side * (keep - recv) if parity else keep + recv
        high, low = split_two(folded)
        for member in range(2):
            part = slice(member * width, (member + 1) * width)
            field_ref[member, :main] = high[:main, part]
            field_ref[member, main : 2 * main] = low[:main, part]
            field_ref[member, 2 * main : 3 * main] = high[:main, part]
            for k, value in enumerate((high, low, high)):
                at = 3 * main + k * tail
                field_ref[member, at : at + tail] = value[main:, part]
            field_ref[member, 3 * main + 3 * tail :] = jnp.zeros((main - 3 * tail, width), BF16)
        count = lax.shift_right_logical(NDEG - first_m - parity + 1, 1)

        def product(member, begin, end):
            table = table_ref[0, parity, begin:end].reshape((end - begin) * padded, table_ref.shape[4])
            table = jnp.concatenate([table[:, :main], table], 1)
            result_ref[member, begin:end] = dot_nn(table, field_ref[member]).reshape(end - begin, padded, width)

        product(0, 0, middle)
        product(1, middle, shares)
        pl.when(count > middle * share)(lambda: product(0, middle, shares))
        pl.when(count < middle * share)(lambda: product(1, middle - 1, middle))

        for local in range(ups):

            @pl.when(lax.rem(step, ups) == local)
            def _():
                begin = (2 * local + parity) * share
                rows = slice(begin, begin + share)
                outs = [mine_ref.at[spot] for spot in range(4)] + [ref.at[i] for ref in cross_refs for i in range(ref.shape[0])]
                for i, out_ref in enumerate(outs):
                    which = 2 * owner_of(i % 4, step, ups, chip, chips) + (core if i < 4 else 1 - core)
                    slot = which * share + lax.broadcasted_iota(jnp.int32, (padded, width), 0)
                    valid = parity + 2 * (slot - count) <= first_m
                    value = jnp.where(slot < count, result_ref[0, which], jnp.where(valid, result_ref[1, which], 0.0))
                    out_ref[rows, :] = value[:share]


def project(place, wave, keeps, recvs, table, share, first, messages):
    half, width = recvs[0].shape[1:]
    shares, padded, depth = table.shape[2:]
    sizes = [recv.shape[0] for recv in recvs]
    starts = [sum(sizes[:i]) for i in range(len(recvs))]
    ups = sum(sizes) // 2
    rows = run_rows(ups, share)

    def field(start, size):
        return pl.BlockSpec((1, half, width), lambda step, *_: (jnp.clip(step - start, 0, size - 1), 0, 0))

    fields = [field(start, size) for start, size in zip(starts, sizes)]
    counts = (shares // 2, *messages)
    return pl.pallas_call(
        functools.partial(project_kernel, share=share, first=first, starts=starts, ups=ups),
        grid_spec=pltpu.PrefetchScalarGridSpec(
            num_scalar_prefetch=2,
            grid=(2 * ups,),
            in_specs=[
                *fields,
                *fields,
                pl.BlockSpec((1,) + table.shape[1:], lambda step, *_: (first + step, 0, 0, 0, 0)),
            ],
            out_specs=[pl.BlockSpec((count, rows, width // 2), lambda step, *_: (0, step // ups, 0)) for count in counts],
            scratch_shapes=[
                pltpu.VMEM((2, 512, width // 2), BF16),
                pltpu.VMEM((2, shares, padded, width // 2), F32),
            ],
        ),
        out_shape=[jax.ShapeDtypeStruct((count, 2 * rows, width // 2), F32) for count in counts],
        compiler_params=pltpu.CompilerParams(vmem_limit_bytes=40 * 1024 * 1024),
        cost_estimate=pl.CostEstimate(flops=10**12, bytes_accessed=10**10, transcendentals=0),
        name="project",
    )(place, wave, *keeps, *recvs, table)


def run_rows(ups, share):
    return (2 * ups * share + 7) // 8 * 8


def energy_kernel(
    place_ref, wave_ref, low_ref, high_ref, far_up_ref, far_down_ref, so_far_ref, out_ref, *, share, first, ways
):
    lanes = out_ref.shape[1]
    halves = []
    for held_ref, far_ref in ((low_ref, far_up_ref), (high_ref, far_down_ref)):
        value = held_ref[...] + far_ref[...]
        squares = value * value
        halves.append(squares[:, :lanes] + squares[:, lanes:])
    squares = jnp.concatenate(halves, 0)
    ones = jnp.ones((8, lanes), BF16)
    squares = sum(dot_nt(ones, piece) for piece in split_three(squares))[:1]

    size = squares.shape[1]
    column = lax.broadcasted_iota(jnp.int32, (1, size), 1)
    start = (2 * place_ref[1] + place_ref[0]) * share
    first_m = jnp.zeros((1, size), jnp.int32)
    parity = jnp.zeros((1, size), jnp.int32)
    slot = jnp.full((1, size), -1, jnp.int32)
    for pair, at in enumerate(ways):
        for s in range(2):
            begin = at + s * share
            inside = (column >= begin) & (column < begin + share)
            first_m = jnp.where(inside, wave_ref[first + pair], first_m)
            parity = jnp.where(inside, s, parity)
            slot = jnp.where(inside, column - begin + start, slot)
    count = lax.shift_right_logical(NDEG - first_m - parity + 1, 1)
    leading = slot < count
    second_m = NDEG - 1 - first_m
    degree = jnp.where(leading, first_m + parity + 2 * slot, second_m + parity + 2 * (slot - count))
    owner_m = jnp.where(leading, first_m, second_m)
    usable = (slot >= 0) & (degree >= 1) & (degree <= NDEG - 1)
    safe = jnp.maximum(degree, 1).astype(F32)
    factor = jnp.where(owner_m == 0, 1.0, 2.0)
    term = jnp.where(usable, factor * squares / (4.0 * safe * (safe + 1.0)), 0.0)
    spot = jnp.where(usable, degree - 1, 0)
    band = lax.broadcasted_iota(jnp.int32, (out_ref.shape[0], size), 0)
    left = jnp.where(lax.shift_right_logical(spot, 7) == band, term, 0.0)
    line = lax.broadcasted_iota(jnp.int32, (lanes, size), 0)
    right = jnp.where((spot & (lanes - 1)) == line, 1.0, 0.0).astype(BF16)
    out_ref[...] = so_far_ref[...] + sum(dot_nt(piece, right) for piece in split_three(left))


def run_energy(place, wave, parts, so_far, share, first, ways):
    rows, width = parts[0].shape
    return pl.pallas_call(
        functools.partial(energy_kernel, share=share, first=first, ways=ways),
        grid_spec=pltpu.PrefetchScalarGridSpec(
            num_scalar_prefetch=2,
            grid=(1,),
            in_specs=own_parts(parts) + [pl.BlockSpec(so_far.shape, lambda step, *_: (0, 0))],
            out_specs=pl.BlockSpec(so_far.shape, lambda step, *_: (0, 0)),
        ),
        out_shape=jax.ShapeDtypeStruct(so_far.shape, F32),
        compiler_params=pltpu.CompilerParams(vmem_limit_bytes=VMEM_SMALL),
        cost_estimate=pl.CostEstimate(flops=10 * rows * width, bytes_accessed=4 * rows * width * 4, transcendentals=0),
        name="run_energy",
    )(place, wave, *parts, so_far)


def own_parts(parts):
    return [pl.BlockSpec(part.shape, lambda step, *_: (0, 0)) for part in parts]


def place_kernel(low_ref, high_ref, far_up_ref, far_down_ref, *refs, share, ways):
    out_ref = refs[-1]
    low = low_ref.shape[0]
    for pair, at in enumerate(ways):
        for parity in range(2):
            begin = at + parity * share
            held_ref, far_ref = (low_ref, far_up_ref) if begin < low else (high_ref, far_down_ref)
            rows = slice(begin % low, begin % low + share)
            value = (held_ref[rows, :] + far_ref[rows, :]).T
            out_ref[pair, parity] = value.reshape(out_ref.shape[2:])


def place_run(parts, held, shape, share, first, ways):
    each = len(ways)
    rows, width = parts[0].shape
    return pl.pallas_call(
        functools.partial(place_kernel, share=share, ways=ways),
        grid=(1,),
        in_specs=own_parts(parts) + [pl.BlockSpec(memory_space=pl.ANY)] * len(held),
        out_specs=pl.BlockSpec((each,) + shape[1:], lambda step: (first // each, 0, 0, 0, 0)),
        out_shape=jax.ShapeDtypeStruct(shape, F32),
        input_output_aliases={len(parts): 0} if held else {},
        compiler_params=pltpu.CompilerParams(vmem_limit_bytes=VMEM_SMALL),
        cost_estimate=pl.CostEstimate(flops=4 * rows * width, bytes_accessed=5 * rows * width * 4, transcendentals=0),
        name="place_run",
    )(*parts, *held)


def all_sum(x):
    for axis, bit in (("band", 1), ("band", 2), ("band", 4), ("wave", 1), ("lev", 1), ("wave", 2), ("wave", 4)):
        size = lax.axis_size(axis)
        x = x + lax.ppermute(x, axis, [(i, i ^ bit) for i in range(size)])
    return x


def shards(fourier, legendre, pair_m, mirror):
    bands = lax.axis_size("band")
    chips = bands // 2
    rows, pairs, members, comps, levs = fourier.shape
    half_rows = rows // 2
    slots = legendre.shape[3]
    share = slots // bands
    padded = (share + 15) // 16 * 16
    position = lax.axis_index("band")
    chip, core = position // 2, position % 2
    place = jnp.stack([core, chip, jnp.int32(chips)]).astype(jnp.int32)

    north_base = position % chips * rows
    south_base = north_base + chips * rows
    partner = lax.dynamic_slice(mirror, (north_base,), (rows,)) - south_base
    plain = (jnp.arange(rows, dtype=jnp.int32) + half_rows) % rows
    index = jnp.where(position < chips, plain, partner).reshape(rows, 1)
    field = jnp.transpose(fourier, (1, 2, 3, 4, 0)).reshape(pairs, members * comps * levs, rows)

    kept, received = [], []
    for i, each in enumerate(MESSAGES):
        message, keep = pick_rows(index, field, sum(MESSAGES[:i]), each)
        kept.append(keep)
        received.append(send_along(message, chips // 2, 0))
        index, legendre, message = lax.optimization_barrier((index, legendre, message))

    table = lay_out(legendre, share, padded)

    firsts = [sum(MESSAGES[: run[0]]) for run in RUNS]
    ways = []
    mine, cross, near, far = {}, {}, {}, {}
    for run in RUNS:
        ups = sum(MESSAGES[i] for i in run) // 2
        ways.append([half * run_rows(ups, share) + 2 * i * share for half in range(2) for i in range(ups)])

    def begin(run, messages, after):
        mine[run], *others = project(
            place, pair_m, [kept[i] for i in RUNS[run]], behind([received[i] for i in RUNS[run]], after), table, share,
            firsts[run], messages,
        )
        cross[run] = [send_along(other, 0, 1) for other in others]

    def send_early(run, after):
        totals = [mine[run][spot] + other[0] for spot, other in enumerate(behind(cross[run][:2], after))]
        near[run] = [send_along(totals[0], 1, 0), send_along(totals[1], -1, 0)]
        return totals

    def send_late(run):
        total, other = mine[run][2], cross[run][2][0]
        low = total.shape[0] // 2
        totals = [
            total[:low] + other[:low] + near[run][0][:low],
            total[low:] + other[low:] + near[run][1][low:],
        ]
        far[run] = [send_along(totals[0], 1, 0), send_along(totals[1], -1, 0)]
        return totals

    begin(0, (1, 1, 1, 1), ())
    begin(1, (1, 1, 2), [send_early(0, ()), cross[0][2:]])
    send_early(1, near[0])
    send_late(0)
    send_late(1)
    shape = (pairs, 2, comps, levs, share)
    held = []
    total = jnp.zeros((16, 128), F32)
    for run in range(len(RUNS)):
        own, other = mine[run][3], cross[run][-1][-1]
        low = own.shape[0] // 2
        parts = [
            own[:low] + other[:low] + near[run][1][:low],
            own[low:] + other[low:] + near[run][0][low:],
            *far[run],
        ]
        total = run_energy(place, pair_m, parts, behind(total, held), share, firsts[run], ways[run])
        held = [place_run(parts, held, shape, share, firsts[run], ways[run])]
    total = all_sum(total)
    return (held[0], jnp.log(total.reshape(-1)[: NDEG - 1]))


def solution(mesh):
    return jax.shard_map(
        shards,
        mesh=mesh,
        in_specs=(
            P("band", "wave", None, None, "lev"),
            P("wave", "band", None, None),
            P("wave"),
            P(),
        ),
        out_specs=(P("wave", None, None, "lev", "band"), P()),
        check_vma=False,
    )
```

```python
import functools

import jax
import jax.numpy as jnp
from jax import lax
from jax.experimental import pallas as pl
from jax.experimental.pallas import tpu as pltpu
from jax.sharding import PartitionSpec as P

NDEG = 1280
MESSAGES = (1, 2, 3, 6)
RUNS = ((0, 1, 2), (3,))
F32 = jnp.float32
BF16 = jnp.bfloat16
VMEM_LIMIT = 56 * 1024 * 1024
VMEM_SMALL = 32 * 1024 * 1024


def behind(x, after):
    return lax.optimization_barrier((x, after))[0]


def split_two(x):
    high = x.astype(BF16)
    low = (x - high.astype(F32)).astype(BF16)
    return high, low


def split_three(x):
    high = x.astype(BF16)
    rest = x - high.astype(F32)
    middle = rest.astype(BF16)
    return high, middle, (rest - middle.astype(F32)).astype(BF16)


def dot_nt(a, b):
    return lax.dot_general(a, b, (((1,), (1,)), ((), ())), preferred_element_type=F32)


def dot_nn(a, b):
    return jnp.dot(a, b, preferred_element_type=F32)


def send_along(x, up, cross):
    size = lax.axis_size("band")
    chips = size // 2
    pairs = [(i, ((i // 2 + up) % chips) * 2 + ((i % 2) ^ cross)) for i in range(size)]
    return lax.ppermute(x, "band", pairs)


def pick_kernel(index_ref, field_ref, send_ref, keep_ref, main_ref, tail_ref):
    count, main = main_ref.shape
    half = count // 2
    rows = field_ref.shape[2]

    @pl.when(pl.program_id(0) == 0)
    def _():
        lanes = lax.broadcasted_iota(jnp.int32, (count, rows), 1)
        chosen = jnp.where(index_ref[...] == lanes, 1.0, 0.0)
        main_ref[...] = chosen[:, :main].astype(BF16)
        tail_ref[...] = jnp.concatenate([chosen[:, main:], chosen[:, main:]], 1).astype(BF16)

    high, low = split_two(field_ref[0])
    tail = jnp.concatenate([high[:, main:], low[:, main:]], 1)
    picked = dot_nt(main_ref[...], high[:, :main]) + dot_nt(main_ref[...], low[:, :main]) + dot_nt(tail_ref[...], tail)
    send_ref[0] = picked[:half]
    keep_ref[0] = picked[half:]


def pick_rows(index, field, first, each):
    pairs, width, rows = field.shape
    count = index.shape[0]
    half = count // 2
    main = 256
    shape = jax.ShapeDtypeStruct((each, half, width), F32)
    out = pl.BlockSpec((1, half, width), lambda step: (step, 0, 0))
    return pl.pallas_call(
        pick_kernel,
        grid=(each,),
        in_specs=[
            pl.BlockSpec((count, 1), lambda step: (0, 0)),
            pl.BlockSpec((1, width, rows), lambda step: (first + step, 0, 0)),
        ],
        out_specs=[out, out],
        out_shape=[shape, shape],
        scratch_shapes=[pltpu.VMEM((count, main), BF16), pltpu.VMEM((count, 2 * (rows - main)), BF16)],
        compiler_params=pltpu.CompilerParams(vmem_limit_bytes=VMEM_LIMIT),
        cost_estimate=pl.CostEstimate(flops=10**12, bytes_accessed=10**10, transcendentals=0),
        name="pick_rows",
    )(index, field)


def layout_kernel(*refs, share):
    out_ref = refs[-1]
    lanes = main = 128
    half = refs[0].shape[1]
    rest = main - 3 * (half - main)
    for parity in range(2):
        for tile, ref in enumerate(refs[:-1]):
            high, low = split_two(ref.reshape(1, 2 * half, lanes)[0, pl.ds(parity, half, stride=2), :])
            blocks = (
                high[:main],
                low[:main],
                jnp.concatenate([high[main:], high[main:], low[main:], jnp.zeros((rest, lanes), BF16)], 0),
            )
            for i, block in enumerate(blocks):
                turned = block.T
                for s in range(out_ref.shape[2]):
                    first = max(s * share, tile * lanes)
                    last = min((s + 1) * share, (tile + 1) * lanes)
                    if first < last:
                        out_ref[0, parity, s, first - s * share : last - s * share, main * i : main * (i + 1)] = turned[
                            first - tile * lanes : last - tile * lanes
                        ]


def lay_out(table, share, padded):
    pairs, half, _, slots = table.shape
    shares = slots // share
    tiles = (slots + 127) // 128

    def block(tile):
        return pl.BlockSpec((1, half, 2, 128), lambda step: (step, 0, 0, tile))

    return pl.pallas_call(
        functools.partial(layout_kernel, share=share),
        grid=(pairs,),
        in_specs=[block(tile) for tile in range(tiles)],
        out_specs=pl.BlockSpec((1, 2, shares, padded, 384), lambda step: (step, 0, 0, 0, 0)),
        out_shape=jax.ShapeDtypeStruct((pairs, 2, shares, padded, 384), BF16),
        compiler_params=pltpu.CompilerParams(vmem_limit_bytes=VMEM_LIMIT),
        cost_estimate=pl.CostEstimate(flops=10**12, bytes_accessed=10**10, transcendentals=0),
        name="lay_out",
    )(*[table] * tiles)


def owner_of(place, step, ups, chip, chips):
    up = jnp.where(step < ups, 1, 0)
    ahead = (1 + up, 2 + up, jnp.where(step < ups, 1, chips - 1), 0)[place]
    return lax.rem(chip + ahead, chips)


def project_kernel(place_ref, wave_ref, *refs, share, first, starts, ups):
    count = len(starts)
    keep_refs, recv_refs = refs[:count], refs[count : 2 * count]
    table_ref, mine_ref, *cross_refs, field_ref, result_ref = refs[2 * count :]
    step = pl.program_id(0)
    core = place_ref[0]
    chip = place_ref[1]
    chips = place_ref[2]
    first_m = wave_ref[first + step]
    half = keep_refs[0].shape[1]
    width = keep_refs[0].shape[2] // 2
    main = 128
    tail = half - main
    shares, padded = table_ref.shape[2:4]
    middle = shares // 2
    side = jnp.where(chip < chips // 2, 1.0, -1.0)
    for parity in range(2):
        keep, recv = keep_refs[0][0], recv_refs[0][0]
        for start, keep_ref, recv_ref in zip(starts[1:], keep_refs[1:], recv_refs[1:]):
            keep = jnp.where(step >= start, keep_ref[0], keep)
            recv = jnp.where(step >= start, recv_ref[0], recv)
        folded = side * (keep - recv) if parity else keep + recv
        high, low = split_two(folded)
        for member in range(2):
            part = slice(member * width, (member + 1) * width)
            field_ref[member, :main] = high[:main, part]
            field_ref[member, main : 2 * main] = low[:main, part]
            field_ref[member, 2 * main : 3 * main] = high[:main, part]
            for k, value in enumerate((high, low, high)):
                at = 3 * main + k * tail
                field_ref[member, at : at + tail] = value[main:, part]
            field_ref[member, 3 * main + 3 * tail :] = jnp.zeros((main - 3 * tail, width), BF16)
        count = lax.shift_right_logical(NDEG - first_m - parity + 1, 1)

        def product(member, begin, end):
            table = table_ref[0, parity, begin:end].reshape((end - begin) * padded, table_ref.shape[4])
            table = jnp.concatenate([table[:, :main], table], 1)
            result_ref[member, begin:end] = dot_nn(table, field_ref[member]).reshape(end - begin, padded, width)

        product(0, 0, middle)
        product(1, middle, shares)
        pl.when(count > middle * share)(lambda: product(0, middle, shares))
        pl.when(count < middle * share)(lambda: product(1, middle - 1, middle))

        for local in range(ups):

            @pl.when(lax.rem(step, ups) == local)
            def _():
                begin = (2 * local + parity) * share
                rows = slice(begin, begin + share)
                outs = [mine_ref.at[spot] for spot in range(4)] + [ref.at[i] for ref in cross_refs for i in range(ref.shape[0])]
                for i, out_ref in enumerate(outs):
                    which = 2 * owner_of(i % 4, step, ups, chip, chips) + (core if i < 4 else 1 - core)
                    slot = which * share + lax.broadcasted_iota(jnp.int32, (padded, width), 0)
                    valid = parity + 2 * (slot - count) <= first_m
                    value = jnp.where(slot < count, result_ref[0, which], jnp.where(valid, result_ref[1, which], 0.0))
                    out_ref[rows, :] = value[:share]


def project(place, wave, keeps, recvs, table, share, first, messages):
    half, width = recvs[0].shape[1:]
    shares, padded, depth = table.shape[2:]
    sizes = [recv.shape[0] for recv in recvs]
    starts = [sum(sizes[:i]) for i in range(len(recvs))]
    ups = sum(sizes) // 2
    rows = run_rows(ups, share)

    def field(start, size):
        return pl.BlockSpec((1, half, width), lambda step, *_: (jnp.clip(step - start, 0, size - 1), 0, 0))

    fields = [field(start, size) for start, size in zip(starts, sizes)]
    counts = (shares // 2, *messages)
    return pl.pallas_call(
        functools.partial(project_kernel, share=share, first=first, starts=starts, ups=ups),
        grid_spec=pltpu.PrefetchScalarGridSpec(
            num_scalar_prefetch=2,
            grid=(2 * ups,),
            in_specs=[
                *fields,
                *fields,
                pl.BlockSpec((1,) + table.shape[1:], lambda step, *_: (first + step, 0, 0, 0, 0)),
            ],
            out_specs=[pl.BlockSpec((count, rows, width // 2), lambda step, *_: (0, step // ups, 0)) for count in counts],
            scratch_shapes=[
                pltpu.VMEM((2, 512, width // 2), BF16),
                pltpu.VMEM((2, shares, padded, width // 2), F32),
            ],
        ),
        out_shape=[jax.ShapeDtypeStruct((count, 2 * rows, width // 2), F32) for count in counts],
        compiler_params=pltpu.CompilerParams(vmem_limit_bytes=40 * 1024 * 1024),
        cost_estimate=pl.CostEstimate(flops=10**12, bytes_accessed=10**10, transcendentals=0),
        name="project",
    )(place, wave, *keeps, *recvs, table)


def run_rows(ups, share):
    return (2 * ups * share + 7) // 8 * 8


def energy_kernel(
    place_ref, wave_ref, low_ref, high_ref, far_up_ref, far_down_ref, so_far_ref, out_ref, *, share, first, ways
):
    lanes = out_ref.shape[1]
    halves = []
    for held_ref, far_ref in ((low_ref, far_up_ref), (high_ref, far_down_ref)):
        value = held_ref[...] + far_ref[...]
        squares = value * value
        halves.append(squares[:, :lanes] + squares[:, lanes:])
    squares = jnp.concatenate(halves, 0)
    ones = jnp.ones((8, lanes), BF16)
    squares = sum(dot_nt(ones, piece) for piece in split_three(squares))[:1]

    size = squares.shape[1]
    column = lax.broadcasted_iota(jnp.int32, (1, size), 1)
    start = (2 * place_ref[1] + place_ref[0]) * share
    first_m = jnp.zeros((1, size), jnp.int32)
    parity = jnp.zeros((1, size), jnp.int32)
    slot = jnp.full((1, size), -1, jnp.int32)
    for pair, at in enumerate(ways):
        for s in range(2):
            begin = at + s * share
            inside = (column >= begin) & (column < begin + share)
            first_m = jnp.where(inside, wave_ref[first + pair], first_m)
            parity = jnp.where(inside, s, parity)
            slot = jnp.where(inside, column - begin + start, slot)
    count = lax.shift_right_logical(NDEG - first_m - parity + 1, 1)
    leading = slot < count
    second_m = NDEG - 1 - first_m
    degree = jnp.where(leading, first_m + parity + 2 * slot, second_m + parity + 2 * (slot - count))
    owner_m = jnp.where(leading, first_m, second_m)
    usable = (slot >= 0) & (degree >= 1) & (degree <= NDEG - 1)
    safe = jnp.maximum(degree, 1).astype(F32)
    factor = jnp.where(owner_m == 0, 1.0, 2.0)
    term = jnp.where(usable, factor * squares / (4.0 * safe * (safe + 1.0)), 0.0)
    spot = jnp.where(usable, degree - 1, 0)
    band = lax.broadcasted_iota(jnp.int32, (out_ref.shape[0], size), 0)
    left = jnp.where(lax.shift_right_logical(spot, 7) == band, term, 0.0)
    line = lax.broadcasted_iota(jnp.int32, (lanes, size), 0)
    right = jnp.where((spot & (lanes - 1)) == line, 1.0, 0.0).astype(BF16)
    out_ref[...] = so_far_ref[...] + sum(dot_nt(piece, right) for piece in split_three(left))


def run_energy(place, wave, parts, so_far, share, first, ways):
    rows, width = parts[0].shape
    return pl.pallas_call(
        functools.partial(energy_kernel, share=share, first=first, ways=ways),
        grid_spec=pltpu.PrefetchScalarGridSpec(
            num_scalar_prefetch=2,
            grid=(1,),
            in_specs=own_parts(parts) + [pl.BlockSpec(so_far.shape, lambda step, *_: (0, 0))],
            out_specs=pl.BlockSpec(so_far.shape, lambda step, *_: (0, 0)),
        ),
        out_shape=jax.ShapeDtypeStruct(so_far.shape, F32),
        compiler_params=pltpu.CompilerParams(vmem_limit_bytes=VMEM_SMALL),
        cost_estimate=pl.CostEstimate(flops=10 * rows * width, bytes_accessed=4 * rows * width * 4, transcendentals=0),
        name="run_energy",
    )(place, wave, *parts, so_far)


def own_parts(parts):
    return [pl.BlockSpec(part.shape, lambda step, *_: (0, 0)) for part in parts]


def place_kernel(low_ref, high_ref, far_up_ref, far_down_ref, *refs, share, ways):
    out_ref = refs[-1]
    low = low_ref.shape[0]
    for pair, at in enumerate(ways):
        for parity in range(2):
            begin = at + parity * share
            held_ref, far_ref = (low_ref, far_up_ref) if begin < low else (high_ref, far_down_ref)
            rows = slice(begin % low, begin % low + share)
            value = (held_ref[rows, :] + far_ref[rows, :]).T
            out_ref[pair, parity] = value.reshape(out_ref.shape[2:])


def place_run(parts, held, shape, share, first, ways):
    each = len(ways)
    rows, width = parts[0].shape
    return pl.pallas_call(
        functools.partial(place_kernel, share=share, ways=ways),
        grid=(1,),
        in_specs=own_parts(parts) + [pl.BlockSpec(memory_space=pl.ANY)] * len(held),
        out_specs=pl.BlockSpec((each,) + shape[1:], lambda step: (first // each, 0, 0, 0, 0)),
        out_shape=jax.ShapeDtypeStruct(shape, F32),
        input_output_aliases={len(parts): 0} if held else {},
        compiler_params=pltpu.CompilerParams(vmem_limit_bytes=VMEM_SMALL),
        cost_estimate=pl.CostEstimate(flops=4 * rows * width, bytes_accessed=5 * rows * width * 4, transcendentals=0),
        name="place_run",
    )(*parts, *held)


def all_sum(x):
    for axis, bit in (("band", 1), ("band", 2), ("band", 4), ("wave", 1), ("lev", 1), ("wave", 2), ("wave", 4)):
        size = lax.axis_size(axis)
        x = x + lax.ppermute(x, axis, [(i, i ^ bit) for i in range(size)])
    return x


def shards(fourier, legendre, pair_m, mirror):
    bands = lax.axis_size("band")
    chips = bands // 2
    rows, pairs, members, comps, levs = fourier.shape
    half_rows = rows // 2
    slots = legendre.shape[3]
    share = slots // bands
    padded = (share + 15) // 16 * 16
    position = lax.axis_index("band")
    chip, core = position // 2, position % 2
    place = jnp.stack([core, chip, jnp.int32(chips)]).astype(jnp.int32)

    north_base = position % chips * rows
    south_base = north_base + chips * rows
    partner = lax.dynamic_slice(mirror, (north_base,), (rows,)) - south_base
    plain = (jnp.arange(rows, dtype=jnp.int32) + half_rows) % rows
    index = jnp.where(position < chips, plain, partner).reshape(rows, 1)
    field = jnp.transpose(fourier, (1, 2, 3, 4, 0)).reshape(pairs, members * comps * levs, rows)

    kept, received = [], []
    for i, each in enumerate(MESSAGES):
        message, keep = pick_rows(index, field, sum(MESSAGES[:i]), each)
        kept.append(keep)
        received.append(send_along(message, chips // 2, 0))
        index, legendre, message = lax.optimization_barrier((index, legendre, message))

    table = lay_out(legendre, share, padded)

    firsts = [sum(MESSAGES[: run[0]]) for run in RUNS]
    ways = []
    mine, cross, near, far = {}, {}, {}, {}
    for run in RUNS:
        ups = sum(MESSAGES[i] for i in run) // 2
        ways.append([half * run_rows(ups, share) + 2 * i * share for half in range(2) for i in range(ups)])

    def begin(run, messages, after):
        mine[run], *others = project(
            place, pair_m, [kept[i] for i in RUNS[run]], behind([received[i] for i in RUNS[run]], after), table, share,
            firsts[run], messages,
        )
        cross[run] = [send_along(other, 0, 1) for other in others]

    def send_early(run, after):
        totals = [mine[run][spot] + other[0] for spot, other in enumerate(behind(cross[run][:2], after))]
        near[run] = [send_along(totals[0], 1, 0), send_along(totals[1], -1, 0)]
        return totals

    def send_late(run):
        total, other = mine[run][2], cross[run][2][0]
        low = total.shape[0] // 2
        totals = [
            total[:low] + other[:low] + near[run][0][:low],
            total[low:] + other[low:] + near[run][1][low:],
        ]
        far[run] = [send_along(totals[0], 1, 0), send_along(totals[1], -1, 0)]
        return totals

    begin(0, (1, 1, 1, 1), ())
    begin(1, (1, 1, 2), [send_early(0, ()), cross[0][2:]])
    send_early(1, near[0])
    send_late(0)
    send_late(1)
    shape = (pairs, 2, comps, levs, share)
    held = []
    total = jnp.zeros((16, 128), F32)
    for run in range(len(RUNS)):
        own, other = mine[run][3], cross[run][-1][-1]
        low = own.shape[0] // 2
        parts = [
            own[:low] + other[:low] + near[run][1][:low],
            own[low:] + other[low:] + near[run][0][low:],
            *far[run],
        ]
        total = run_energy(place, pair_m, parts, behind(total, held), share, firsts[run], ways[run])
        held = [place_run(parts, held, shape, share, firsts[run], ways[run])]
    total = all_sum(total)
    return (held[0], jnp.log(total.reshape(-1)[: NDEG - 1]))


def solution(mesh):
    return jax.shard_map(
        shards,
        mesh=mesh,
        in_specs=(
            P("band", "wave", None, None, "lev"),
            P("wave", "band", None, None),
            P("wave"),
            P(),
        ),
        out_specs=(P("wave", None, None, "lev", "band"), P()),
        check_vma=False,
    )
```
